256 devices in a mesh: gx: 32 (over x, y, core), gy: 8 (over z).
Axes of the slice: x: 4, y: 4, z: 8, core: 2. Of those that a mesh axis runs over, the one named last changes fastest.
Arguments:
- cotangent: float32 [256, 512, 512], P('gx', 'gy'), may hold values from -6 to 6
- coefficient: float32 [256, 512, 512], P('gx', 'gy'), may hold values from 0.5 to 6
Outputs:
- rhs_cotangent: float32 [256, 512, 512], P('gx', 'gy')
The draws below stay inside these ranges and needn't reach their ends.
All inputs are finite; a program needn't handle non-finite values.
Results may differ from the reference program's by a relative error of at most 0.00024.
Values sent between devices are 32-bit elements; how exact they have to be, the bound alone decides.
No kernel may reach another device: no remote copies, remote signals or barrier semaphores. Data moves between devices by JAX's collectives and lax.ppermute only.
A program may use at most 64 MiB of HBM per device.

```python
import math
import jax
import jax.numpy as jnp

NX = 256
NY = 512
NZ = 512


def block_levels(key, shape, pieces, low, high):
    factor_of = 1.0
    for axis_at, shards_of in pieces:
        draws = jax.random.uniform(jax.random.fold_in(jax.random.fold_in(key, 6), axis_at), (shards_of,), jnp.float32, low / len(pieces), high / len(pieces))
        factor_of = factor_of * jnp.repeat(jnp.exp(draws), shape[axis_at] // shards_of).reshape((-1,) + (1,) * (len(shape) - 1 - axis_at))
    return factor_of


def gaussian(rng, shape, width, bound, split=(), dtype=jnp.bfloat16):
    loudness = block_levels(rng, shape, split, -0.22, 0.18) if split else 1.0
    result = jax.random.normal(rng, shape, jnp.float32) * width * loudness
    return jnp.minimum(jnp.maximum(result, -bound), bound).astype(dtype)


def setup_inputs(seed: int = 0) -> dict:
    key_list = jax.random.split(jax.random.key(seed), 3)
    cotangent = gaussian(key_list[0], (NX, NY, NZ), 1.0, 6.0, ((0, 32), (1, 8)), jnp.float32)
    coefficient = jnp.clip(jnp.exp(math.log(6.0) - 2.4849066 * jax.random.uniform(key_list[1], (NX, NY, NZ), jnp.float32) ** block_levels(key_list[1], (NX, NY, NZ), ((0, 32), (1, 8)), -0.2, 0.2)), 0.5, 6.0)
    return dict(cotangent=cotangent, coefficient=coefficient)


screen = 0.02
first_weight = 1.0 / (1.25 + 0.75 * math.cos(math.pi / 4.0))
second_weight = 1.0 / (1.25 - 0.75 * math.cos(math.pi / 4.0))


def operate(field, coefficient):
    beside = jnp.roll(field, 1, 0) + jnp.roll(field, -1, 0)
    beside = beside + jnp.roll(field, 1, 1) + jnp.roll(field, -1, 1)
    beside = beside + jnp.roll(field, 1, 2) + jnp.roll(field, -1, 2)
    return (6.0 + coefficient) * field - beside


def symbol(length):
    freq = jnp.arange(length).astype(jnp.float32)
    return 2.0 - 2.0 * jnp.cos(2.0 * math.pi * freq / length)


def coarse_solve(sums):
    size_x, size_y, size_z = sums.shape
    spectrum = screen + symbol(size_x)[:, None, None] + symbol(size_y)[None, :, None] + symbol(size_z)[None, None, :]
    return jnp.real(jnp.fft.ifftn(jnp.fft.fftn(sums) / spectrum)).astype(jnp.float32)


def reference(cotangent, coefficient):
    inverse = 1.0 / (6.0 + coefficient)
    weight_five = second_weight * cotangent * inverse
    carried_four = cotangent - operate(weight_five, coefficient)
    weight_four = first_weight * carried_four * inverse
    carried_three = carried_four - operate(weight_four, coefficient)
    size_x, size_y, size_z = carried_three.shape
    block_sums = carried_three.reshape(size_x // 8, 8, size_y // 8, 8, size_z // 8, 8).sum(axis=(1, 3, 5))
    coarse = coarse_solve(block_sums)
    spread = jnp.broadcast_to(coarse[:, None, :, None, :, None], (size_x // 8, 8, size_y // 8, 8, size_z // 8, 8))
    spread = spread.reshape(size_x, size_y, size_z) / 8.0
    carried_two = carried_three - operate(spread, coefficient)
    weight_two = second_weight * carried_two * inverse
    carried_one = carried_two - operate(weight_two, coefficient)
    return weight_five + weight_four + spread + weight_two + first_weight * carried_one * inverse
```

```python
import functools
import math

import jax
import jax.numpy as jnp
import numpy as np
from jax import lax
from jax.experimental import pallas as pl
from jax.experimental.pallas import tpu as pltpu
from jax.sharding import Mesh
from jax.sharding import PartitionSpec as P

screen = 0.02
w1 = 1.0 / (1.25 + 0.75 * math.cos(math.pi / 4.0))
w2 = 1.0 / (1.25 - 0.75 * math.cos(math.pi / 4.0))

BX, BY, NZ = 8, 64, 512
CX, CY, CZ = 32, 64, 64
GX, GY = 32, 8
CHIPS = GX // 2
ROWS = CY // 2
OUT_Y = BY // 8 + 2
OUT_X = 4

VMEM = pl.BlockSpec(memory_space=pltpu.VMEM)
SMEM = pl.BlockSpec(memory_space=pltpu.SMEM)
F32 = jnp.float32


def basis():
    place = np.arange(CZ)
    columns, freq = [], []
    for k in range(CZ // 2 + 1):
        scale = math.sqrt((1.0 if k in (0, CZ // 2) else 2.0) / CZ)
        columns.append(scale * np.cos(2.0 * math.pi * k * place / CZ))
        freq.append(k)
    for k in range(1, CZ // 2):
        columns.append(math.sqrt(2.0 / CZ) * np.sin(2.0 * math.pi * k * place / CZ))
        freq.append(k)
    return np.stack(columns, 1), np.array(freq)


def symbol(length):
    return 2.0 - 2.0 * np.cos(2.0 * math.pi * np.arange(length) / length)


def tables():
    columns, freq = basis()
    spectrum = (
        screen
        + symbol(CX)[:, None, None]
        + symbol(CY)[None, :, None]
        + symbol(CZ)[freq][None, None, :]
    )
    green = np.real(np.fft.ifft2(1.0 / spectrum, axes=(0, 1)))
    d, r, h = np.meshgrid(np.arange(GY), np.arange(4), np.arange(2), indexing="ij")
    slabs = []
    for j in range(-1, OUT_Y - 1):
        shift = (j - (8 * d + 4 * h + r)) % CY
        slabs.append(green[: CX // 2 + 1][:, shift].reshape(CX // 2 + 1, ROWS, 2 * CZ))
    table = np.stack(slabs, 1).astype(np.float32)
    into = np.repeat(columns, NZ // CZ, axis=0).astype(np.float32)
    out = np.concatenate([into.T, into.T], 0) / 8.0
    return table, into, out.astype(np.float32)


def zsum(v):
    return pltpu.roll(v, 1, 1) + pltpu.roll(v, NZ - 1, 1)


def shifted_sum(v, low, high):
    size = v.shape[0]
    row = lax.broadcasted_iota(jnp.int32, v.shape, 0)
    before = jnp.where(row == 0, low, pltpu.roll(v, 1, 0))
    after = jnp.where(row == size - 1, high, pltpu.roll(v, size - 1, 0))
    return before + after


def pack_kernel(core_ref, cot_ref, coef_ref, near_ref, far_ref, tnear_ref, tfar_ref, ylow_ref, yhigh_ref):
    core = core_ref[0]
    edges = (
        (near_ref, tnear_ref, (BX - 1) * (1 - core), 2 * core - 1),
        (far_ref, tfar_ref, (BX - 1) * core, 1 - 2 * core),
    )
    for out, tiny, edge, step in edges:
        cot = cot_ref[edge]
        inverse = 1.0 / (6.0 + coef_ref[edge])
        w5 = w2 * cot * inverse
        tiny[0:1, :] = w5[0:1, :]
        tiny[1:2, :] = w5[BY - 1 : BY, :]
        out[0] = w5
        out[1] = inverse
        out[2] = (1.0 - w2) * cot + w2 * cot_ref[edge + step] / (6.0 + coef_ref[edge + step])
    for out, edge, inner in ((ylow_ref, 0, 1), (yhigh_ref, BY - 1, BY - 2)):
        cot = cot_ref[:, edge, :]
        inverse = 1.0 / (6.0 + coef_ref[:, edge, :])
        out[0:8, :] = w2 * cot * inverse
        out[8:16, :] = inverse
        out[16:24, :] = (1.0 - w2) * cot + w2 * cot_ref[:, inner, :] / (6.0 + coef_ref[:, inner, :])


def first_kernel(
    core_ref, cot_ref, coef_ref, near_ref, far_ref, ylow_ref, yhigh_ref, into_ref,
    c3_ref, base_ref, inverse_ref, cnear_ref, cfar_ref, cylow_ref, cyhigh_ref, send_ref,
    w5_ref, w4_ref,
):
    core = core_ref[0]
    halos = ((near_ref, (BX + 1) * (1 - core), core == 0), (far_ref, (BX + 1) * core, core == 1))
    for x in range(BX):
        inverse = 1.0 / (6.0 + coef_ref[x])
        inverse_ref[x] = inverse
        w5_ref[x + 1] = w2 * cot_ref[x] * inverse
    for halo, place, _ in halos:
        w5_ref[place] = halo[0]
    y4 = []
    for packet, edge in ((ylow_ref, 0), (yhigh_ref, BY - 1)):
        w5 = packet[0:8, :]
        c4 = packet[16:24, :] + w5_ref[1 : BX + 1, edge, :] + zsum(w5)
        c4 = c4 + shifted_sum(w5, packet[24:25, :], packet[25:26, :])
        y4.append(w1 * packet[8:16, :] * c4)
    for halo, place, at_high in halos:
        inner = jnp.where(at_high, BX, 1)
        low = jnp.where(at_high, ylow_ref[25:26, :], ylow_ref[24:25, :])
        high = jnp.where(at_high, yhigh_ref[25:26, :], yhigh_ref[24:25, :])
        w5 = halo[0]
        c4 = halo[2] + w5_ref[inner] + zsum(w5) + shifted_sum(w5, low, high)
        w4_ref[place] = w1 * halo[1] * c4
    for x in range(BX):
        w5 = w5_ref[x + 1]
        c4 = (1.0 - w2) * cot_ref[x] + w5_ref[x] + w5_ref[x + 2] + zsum(w5)
        c4 = c4 + shifted_sum(w5, ylow_ref[x : x + 1, :], yhigh_ref[x : x + 1, :])
        w4 = w1 * inverse_ref[x] * c4
        w4_ref[x + 1] = w4
        base_ref[x] = w5 + w4
        c3_ref[x] = c4
    total = jnp.zeros((BY, NZ), F32)
    for x in range(BX):
        w4 = w4_ref[x + 1]
        c3 = (1.0 - w1) * c3_ref[x] + w4_ref[x] + w4_ref[x + 2] + zsum(w4)
        c3 = c3 + shifted_sum(w4, y4[0][x : x + 1, :], y4[1][x : x + 1, :])
        c3_ref[x] = c3
        cylow_ref[x : x + 1, :] = c3[0:1, :]
        cyhigh_ref[x : x + 1, :] = c3[BY - 1 : BY, :]
        total = total + c3
    sums = jnp.sum(total.reshape(BY // 8, 8, NZ), axis=1)
    modes = jnp.dot(sums, into_ref[...], precision=lax.Precision.HIGHEST, preferred_element_type=F32)
    packed = jnp.concatenate([modes[0:4, :], modes[4:8, :]], axis=1)
    send_ref[...] = jnp.broadcast_to(packed[None], send_ref.shape)
    cnear_ref[...] = c3_ref[(BX - 1) * (1 - core)]
    cfar_ref[...] = c3_ref[(BX - 1) * core]


def coarse_kernel(place_ref, got_ref, table_ref, own_ref, other_ref, rolled_ref):
    core, chip, gy = place_ref[0], place_ref[1], place_ref[2]
    turn = lax.rem(ROWS - 4 * gy, ROWS)
    for q in range(CHIPS):
        plane = lax.rem(chip + (1 - 2 * core) * q + CHIPS, CHIPS)
        rolled_ref[q] = pltpu.roll(got_ref[plane], turn, 0)

    def step(q, totals):
        totals = list(totals)
        for m in range(-1, OUT_X - 1):
            away = lax.rem(2 * CX - 2 * q + m, CX)
            away = jnp.minimum(away, CX - away)
            for j in range(OUT_Y):
                at = (m + 1) * OUT_Y + j
                for part in range(ROWS // 8):
                    rows = slice(8 * part, 8 * part + 8)
                    totals[at] = totals[at] + table_ref[away, j, rows, :] * rolled_ref[q, rows, :]
        return tuple(totals)

    zero = jnp.zeros((8, 2 * CZ), F32)
    totals = lax.fori_loop(0, CHIPS, step, (zero,) * (OUT_X * OUT_Y))
    for m in range(3):
        for j in range(OUT_Y):
            at = m * OUT_Y + j
            own_ref[at : at + 1, :] = jnp.sum(totals[at], axis=0, keepdims=True)
            at_other = (OUT_X - 1 - m) * OUT_Y + j
            other_ref[at : at + 1, :] = jnp.sum(totals[at_other], axis=0, keepdims=True)


def last_kernel(
    core_ref, own_ref, other_ref, out_table_ref, c3_ref, base_ref, inverse_ref,
    cnear_ref, cfar_ref, near_ref, far_ref, cylow_ref, cyhigh_ref, ylow_ref, yhigh_ref,
    out_ref, w_ref,
):
    core = core_ref[0]
    modes = own_ref[...] + other_ref[...]
    coarse = jnp.dot(modes, out_table_ref[...], precision=lax.Precision.HIGHEST, preferred_element_type=F32)
    outer, middle, inner = (coarse[m * OUT_Y : (m + 1) * OUT_Y, :] for m in range(3))
    low = jnp.where(core == 0, outer, inner)
    high = jnp.where(core == 0, inner, outer)

    def rows_of(plane):
        return jnp.concatenate([jnp.broadcast_to(plane[j : j + 1, :], (8, NZ)) for j in range(1, OUT_Y - 1)], 0)

    def side_sum(plane, fine):
        return shifted_sum(fine, plane[0:1, :], plane[OUT_Y - 1 : OUT_Y, :]) + zsum(fine)

    s, s_low, s_high = rows_of(middle), rows_of(low), rows_of(high)
    beside = side_sum(middle, s)
    for fine, plane, is_low in ((s_low, low, True), (s_high, high, False)):
        c3 = jnp.where((core == 0) == is_low, cfar_ref[...], cnear_ref[...])
        inverse = jnp.where((core == 0) == is_low, far_ref[1], near_ref[1])
        value = c3 + fine + s + side_sum(plane, fine)
        w_ref[0 if is_low else BX + 1] = w2 * (inverse * value - fine)
    y_w = []
    for c3_rows, packet, edge, near_edge in (
        (cylow_ref, ylow_ref, 0, 1),
        (cyhigh_ref, yhigh_ref, OUT_Y - 1, OUT_Y - 2),
    ):
        fine = jnp.broadcast_to(middle[edge : edge + 1, :], (BX, NZ))
        value = c3_rows[...] + fine + middle[near_edge : near_edge + 1, :] + zsum(fine)
        value = value + shifted_sum(fine, low[edge : edge + 1, :], high[edge : edge + 1, :])
        y_w.append(w2 * (packet[8:16, :] * value - fine))
    for x in range(BX):
        around = beside + (s_low if x == 0 else s) + (s_high if x == BX - 1 else s)
        w_ref[x + 1] = w2 * (inverse_ref[x] * (c3_ref[x] + around) - s)
    for x in range(BX):
        w = w_ref[x + 1]
        inverse = inverse_ref[x]
        near = w_ref[x] + w_ref[x + 2] + zsum(w)
        near = near + shifted_sum(w, y_w[0][x : x + 1, :], y_w[1][x : x + 1, :])
        out_ref[x] = base_ref[x] + s + w + w1 * ((1.0 - w2) / w2 * w + inverse * near)


def call(kernel, outs, ins, scratch=(), smem=1):
    return pl.pallas_call(
        kernel,
        out_shape=[jax.ShapeDtypeStruct(shape, F32) for shape in outs],
        in_specs=[SMEM] * smem + [VMEM] * (len(ins) - smem),
        out_specs=[VMEM] * len(outs),
        scratch_shapes=[pltpu.VMEM(shape, F32) for shape in scratch],
        compiler_params=pltpu.CompilerParams(vmem_limit_bytes=40 * 1024 * 1024),
    )(*ins)


def body(cotangent, coefficient):
    table, into, out_table = tables()
    along_x = ("x", "y", "core")
    core = lax.axis_index("core")
    place = jnp.stack([core, lax.axis_index("x") * 4 + lax.axis_index("y"), lax.axis_index("gy")])
    place = place.astype(jnp.int32)
    near_pairs = [(i, i ^ 1) for i in range(GX)]
    far_pairs = [(i, (i + 1) % GX if i % 2 else (i - 1) % GX) for i in range(GX)]
    up = [(i, (i + 1) % GY) for i in range(GY)]
    down = [(i, (i - 1) % GY) for i in range(GY)]

    def near_swap(v):
        return lax.ppermute(v, along_x, near_pairs)

    def far_swap(v):
        return lax.ppermute(v, along_x, far_pairs)

    plane, rows = (BY, NZ), (BX, NZ)
    near, far, tiny_near, tiny_far, y_low, y_high = call(
        pack_kernel,
        [(3,) + plane, (3,) + plane, (2, NZ), (2, NZ), (24, NZ), (24, NZ)],
        [place, cotangent, coefficient],
    )
    tiny_near, tiny_far = near_swap(tiny_near), far_swap(tiny_far)
    near, far = near_swap(near), far_swap(far)
    corner_low = jnp.where(core == 0, tiny_far, tiny_near)
    corner_high = jnp.where(core == 0, tiny_near, tiny_far)
    y_low = jnp.concatenate([y_low, corner_low[0:1], corner_high[0:1]], 0)
    y_high = jnp.concatenate([y_high, corner_low[1:2], corner_high[1:2]], 0)
    from_low = lax.ppermute(y_high, "gy", up)
    from_high = lax.ppermute(y_low, "gy", down)
    brick = (BX, BY, NZ)
    c3, base, inverse, c_near, c_far, cy_low, cy_high, send = call(
        first_kernel,
        [brick, brick, brick, plane, plane, rows, rows, (CHIPS * GY, 4, 2 * CZ)],
        [place, cotangent, coefficient, near, far, from_low, from_high, jnp.asarray(into)],
        scratch=[(BX + 2,) + plane, (BX + 2,) + plane],
    )
    got = lax.all_to_all(send, ("x", "y", "gy"), 0, 0, tiled=True)
    c_near, c_far = near_swap(c_near), far_swap(c_far)
    c_from_low = lax.ppermute(cy_high, "gy", up)
    c_from_high = lax.ppermute(cy_low, "gy", down)
    own, other = call(
        coarse_kernel,
        [(3 * OUT_Y, 2 * CZ), (3 * OUT_Y, 2 * CZ)],
        [place, got.reshape(CHIPS, ROWS, 2 * CZ), jnp.asarray(table)],
        scratch=[(CHIPS, ROWS, 2 * CZ)],
    )
    other = near_swap(other)
    return call(
        last_kernel,
        [brick],
        [
            place, own, other, jnp.asarray(out_table), c3, base, inverse,
            c_near, c_far, near, far, c_from_low, c_from_high, from_low, from_high,
        ],
        scratch=[(BX + 2,) + plane],
    )[0]


def solution(mesh):
    split = Mesh(np.asarray(mesh.devices).reshape(4, 4, 2, GY), ("x", "y", "core", "gy"))
    spec = P(("x", "y", "core"), "gy", None)
    return jax.shard_map(body, mesh=split, in_specs=(spec, spec), out_specs=spec, check_vma=False)
```

```python
import math

import jax
import jax.numpy as jnp
import numpy as np
from jax import lax
from jax.experimental import pallas as pl
from jax.experimental.pallas import tpu as pltpu
from jax.sharding import Mesh
from jax.sharding import PartitionSpec as P

screen = 0.02
w1 = 1.0 / (1.25 + 0.75 * math.cos(math.pi / 4.0))
w2 = 1.0 / (1.25 - 0.75 * math.cos(math.pi / 4.0))

BX, BY, NZ = 8, 64, 512
CX, CY, CZ = 32, 64, 64
GX, GY = 32, 8
CHIPS = GX // 2
ROWS = CY // 2
OUT_Y = BY // 8 + 2
OUT_X = 4

VMEM = pl.BlockSpec(memory_space=pltpu.VMEM)
SMEM = pl.BlockSpec(memory_space=pltpu.SMEM)
HBM = pl.BlockSpec(memory_space=pltpu.HBM)
F32 = jnp.float32


def basis():
    place = np.arange(CZ)
    columns, freq = [], []
    for k in range(CZ // 2 + 1):
        scale = math.sqrt((1.0 if k in (0, CZ // 2) else 2.0) / CZ)
        columns.append(scale * np.cos(2.0 * math.pi * k * place / CZ))
        freq.append(k)
    for k in range(1, CZ // 2):
        columns.append(math.sqrt(2.0 / CZ) * np.sin(2.0 * math.pi * k * place / CZ))
        freq.append(k)
    return np.stack(columns, 1), np.array(freq)


def symbol(length):
    return 2.0 - 2.0 * np.cos(2.0 * math.pi * np.arange(length) / length)


def tables():
    columns, freq = basis()
    spectrum = (
        screen
        + symbol(CX)[:, None, None]
        + symbol(CY)[None, :, None]
        + symbol(CZ)[freq][None, None, :]
    )
    green = np.real(np.fft.ifft2(1.0 / spectrum, axes=(0, 1)))
    t, d, h = np.meshgrid(np.arange(OUT_Y + 3), np.arange(GY), np.arange(2), indexing="ij")
    shift = (t - 4 - 8 * d - 4 * h) % CY
    table = green[: CX // 2 + 1][:, shift].reshape(CX // 2 + 1, OUT_Y + 3, GY, 2 * CZ)
    table = table.astype(np.float32)
    into = np.repeat(columns, NZ // CZ, axis=0).astype(np.float32)
    out = np.concatenate([into.T, into.T], 0) / 8.0
    return table, into, out.astype(np.float32)


def zsum(v):
    return pltpu.roll(v, 1, 1) + pltpu.roll(v, NZ - 1, 1)


def shifted_sum(v, low, high):
    size = v.shape[0]
    row = lax.broadcasted_iota(jnp.int32, v.shape, 0)
    before = jnp.where(row == 0, low, pltpu.roll(v, 1, 0))
    after = jnp.where(row == size - 1, high, pltpu.roll(v, size - 1, 0))
    return before + after


def fetch(pairs, sems, first=0):
    copies = [pltpu.make_async_copy(s, d, sems.at[first + i]) for i, (s, d) in enumerate(pairs)]
    for copy in copies:
        copy.start()
    return copies


def wait(copies):
    for copy in copies:
        copy.wait()


def pack_kernel(
    core_ref, cot_hbm, coef_hbm,
    near_ref, far_ref, tnear_ref, tfar_ref, ylow_ref, yhigh_ref, cot_ref, coef_ref, sems,
):
    core = core_ref[0]
    order = (0, 1, BX - 2, BX - 1) + tuple(range(2, BX - 2))
    copies = fetch(
        [(a.at[x], b.at[x]) for x in order for a, b in ((cot_hbm, cot_ref), (coef_hbm, coef_ref))],
        sems,
    )
    wait(copies[:8])
    edges = (
        (near_ref, tnear_ref, (BX - 1) * (1 - core), 2 * core - 1),
        (far_ref, tfar_ref, (BX - 1) * core, 1 - 2 * core),
    )
    for out, tiny, edge, step in edges:
        cot = cot_ref[edge]
        inverse = 1.0 / (6.0 + coef_ref[edge])
        w5 = w2 * cot * inverse
        tiny[0:1, :] = w5[0:1, :]
        tiny[1:2, :] = w5[BY - 1 : BY, :]
        out[0] = w5
        out[1] = inverse
        out[2] = (1.0 - w2) * cot + w2 * cot_ref[edge + step] / (6.0 + coef_ref[edge + step])
    wait(copies[8:])
    for out, edge, inner in ((ylow_ref, 0, 1), (yhigh_ref, BY - 1, BY - 2)):
        cot = cot_ref[:, edge, :]
        inverse = 1.0 / (6.0 + coef_ref[:, edge, :])
        out[0:8, :] = w2 * cot * inverse
        out[8:16, :] = inverse
        out[16:24, :] = (1.0 - w2) * cot + w2 * cot_ref[:, inner, :] / (6.0 + coef_ref[:, inner, :])


def local_kernel(cot_ref, coef_ref, w5_ref, inverse_ref, c4_ref):
    for x in range(BX):
        inverse = 1.0 / (6.0 + coef_ref[x])
        inverse_ref[x] = inverse
        w5_ref[x] = w2 * cot_ref[x] * inverse
    none = jnp.zeros((1, NZ), F32)
    for x in range(BX):
        w5 = w5_ref[x]
        c4 = (1.0 - w2) * cot_ref[x] + zsum(w5) + shifted_sum(w5, none, none)
        if x > 0:
            c4 = c4 + w5_ref[x - 1]
        if x < BX - 1:
            c4 = c4 + w5_ref[x + 1]
        c4_ref[x] = c4


def first_kernel(
    core_ref, w5_ref, inverse_ref, part_ref, near_ref, far_ref, ylow_ref, yhigh_ref, into_hbm,
    c3_hbm, base_hbm, inverse_hbm, planes_hbm, rows_hbm,
    cnear_ref, cfar_ref, cylow_ref, cyhigh_ref, send_ref,
    halo_ref, w4_ref, c3_ref, base_ref, into_ref, sems,
):
    core = core_ref[0]
    copies = fetch(
        [(into_hbm, into_ref)]
        + [(inverse_ref.at[x], inverse_hbm.at[x]) for x in range(BX)]
        + [
            (near_ref.at[1], planes_hbm.at[1 - core]),
            (far_ref.at[1], planes_hbm.at[core]),
            (ylow_ref.at[pl.ds(8, 8)], rows_hbm.at[0]),
            (yhigh_ref.at[pl.ds(8, 8)], rows_hbm.at[1]),
        ],
        sems,
    )
    halos = ((near_ref, 1 - core, core == 0), (far_ref, core, core == 1))
    y4 = []
    for packet, edge in ((ylow_ref, 0), (yhigh_ref, BY - 1)):
        w5 = packet[0:8, :]
        c4 = packet[16:24, :] + w5_ref[:, edge, :] + zsum(w5)
        c4 = c4 + shifted_sum(w5, packet[24:25, :], packet[25:26, :])
        y4.append(w1 * packet[8:16, :] * c4)
    for halo, side, at_high in halos:
        halo_ref[side] = halo[0]
        low = jnp.where(at_high, ylow_ref[25:26, :], ylow_ref[24:25, :])
        high = jnp.where(at_high, yhigh_ref[25:26, :], yhigh_ref[24:25, :])
        w5 = halo[0]
        c4 = halo[2] + w5_ref[(BX - 1) * side] + zsum(w5) + shifted_sum(w5, low, high)
        w4_ref[(BX + 1) * side] = w1 * halo[1] * c4
    row = lax.broadcasted_iota(jnp.int32, (8, NZ), 0)
    for x in range(BX):
        low = jnp.where(row == 0, ylow_ref[x : x + 1, :], 0.0)
        high = jnp.where(row == 7, yhigh_ref[x : x + 1, :], 0.0)
        part = part_ref[x]
        c4 = jnp.concatenate([part[0:8, :] + low, part[8 : BY - 8, :], part[BY - 8 : BY, :] + high], 0)
        if x == 0:
            c4 = c4 + halo_ref[0]
        if x == BX - 1:
            c4 = c4 + halo_ref[1]
        w4 = w1 * inverse_ref[x] * c4
        w4_ref[x + 1] = w4
        base_ref[x] = w5_ref[x] + w4
        c3_ref[x] = c4
        copies += fetch([(base_ref.at[x], base_hbm.at[x])], sems, BX + 5 + x)
    total = jnp.zeros((BY, NZ), F32)
    for x in range(BX):
        w4 = w4_ref[x + 1]
        c3 = (1.0 - w1) * c3_ref[x] + w4_ref[x] + w4_ref[x + 2] + zsum(w4)
        c3 = c3 + shifted_sum(w4, y4[0][x : x + 1, :], y4[1][x : x + 1, :])
        c3_ref[x] = c3
        copies += fetch([(c3_ref.at[x], c3_hbm.at[x])], sems, 2 * BX + 5 + x)
        cylow_ref[x : x + 1, :] = c3[0:1, :]
        cyhigh_ref[x : x + 1, :] = c3[BY - 1 : BY, :]
        total = total + c3
    sums = jnp.sum(total.reshape(BY // 8, 8, NZ), axis=1)
    copies[0].wait()
    modes = jnp.dot(sums, into_ref[...], precision=lax.Precision.HIGHEST, preferred_element_type=F32)
    packed = jnp.concatenate([modes[0:4, :], modes[4:8, :]], axis=1)
    send_ref[...] = jnp.broadcast_to(packed[None], send_ref.shape)
    cnear_ref[...] = c3_ref[(BX - 1) * (1 - core)]
    cfar_ref[...] = c3_ref[(BX - 1) * core]
    wait(copies[1:])


def coarse_kernel(
    place_ref, got_ref, table_hbm, out_table_hbm, c3_hbm, base_hbm, inverse_hbm, planes_hbm, rows_hbm,
    cnear_hbm, cfar_hbm, cylow_hbm, cyhigh_hbm,
    own_ref, other_ref, out_table_ref, c3_ref, base_ref, inverse_ref, planes_ref, rows_ref,
    cplanes_ref, crows_ref, table_ref, rolled_ref, sums_ref, sems,
):
    core, chip, gy = place_ref[0], place_ref[1], place_ref[2]
    first = fetch([(table_hbm.at[i], table_ref.at[i]) for i in range(CX // 2 + 1)], sems)
    later = fetch(
        [(a.at[x], b.at[x]) for a, b in ((c3_hbm, c3_ref), (inverse_hbm, inverse_ref)) for x in range(BX)]
        + [
            (out_table_hbm, out_table_ref),
            (planes_hbm, planes_ref),
            (rows_hbm, rows_ref),
            (cnear_hbm, cplanes_ref.at[1 - core]),
            (cfar_hbm, cplanes_ref.at[core]),
            (cylow_hbm, crows_ref.at[0]),
            (cyhigh_hbm, crows_ref.at[1]),
        ]
        + [(base_hbm.at[x], base_ref.at[x]) for x in range(BX)],
        sems,
        CX // 2 + 1,
    )
    turn = lax.rem(GY - gy, GY)
    for q in range(CHIPS):
        plane = lax.rem(chip + (1 - 2 * core) * q + CHIPS, CHIPS)
        for r in range(4):
            rolled_ref[q, r] = pltpu.roll(got_ref[plane, pl.ds(r, GY, stride=4), :], turn, 0)
    wait(first)

    def step(q, totals):
        totals = list(totals)
        source = [rolled_ref[q, r] for r in range(4)]
        for m in range(-1, OUT_X - 1):
            away = lax.rem(2 * CX - 2 * q + m, CX)
            away = jnp.minimum(away, CX - away)
            weight = [table_ref[away, t] for t in range(OUT_Y + 3)]
            for j in range(OUT_Y):
                at = (m + 1) * OUT_Y + j
                for r in range(4):
                    totals[at] = totals[at] + weight[j + 3 - r] * source[r]
        return tuple(totals)

    zero = jnp.zeros((8, 2 * CZ), F32)
    totals = lax.fori_loop(0, CHIPS, step, (zero,) * (OUT_X * OUT_Y), unroll=2)
    for at in range(OUT_X * OUT_Y):
        sums_ref[at : at + 1, :] = jnp.sum(totals[at], axis=0, keepdims=True)
    own_ref[...] = sums_ref[0 : 3 * OUT_Y, :]
    for m in range(3):
        start = (OUT_X - 1 - m) * OUT_Y
        other_ref[m * OUT_Y : (m + 1) * OUT_Y, :] = sums_ref[start : start + OUT_Y, :]
    wait(later)


def last_kernel(
    core_ref, own_ref, other_ref, out_table_ref, c3_ref, base_ref, inverse_ref, planes_ref, rows_ref,
    cplanes_ref, crows_ref,
    out_hbm, w_ref, out_ref, sems,
):
    core = core_ref[0]
    modes = own_ref[...] + other_ref[...]
    coarse = jnp.dot(modes, out_table_ref[...], precision=lax.Precision.HIGHEST, preferred_element_type=F32)
    outer, middle, inner = (coarse[m * OUT_Y : (m + 1) * OUT_Y, :] for m in range(3))
    low = jnp.where(core == 0, outer, inner)
    high = jnp.where(core == 0, inner, outer)

    def rows_of(plane):
        return jnp.concatenate([jnp.broadcast_to(plane[j : j + 1, :], (8, NZ)) for j in range(1, OUT_Y - 1)], 0)

    def side_sum(plane, fine):
        return shifted_sum(fine, plane[0:1, :], plane[OUT_Y - 1 : OUT_Y, :]) + zsum(fine)

    s, s_low, s_high = rows_of(middle), rows_of(low), rows_of(high)
    beside = side_sum(middle, s)
    for side, fine, plane in ((0, s_low, low), (1, s_high, high)):
        value = cplanes_ref[side] + fine + s + side_sum(plane, fine)
        w_ref[(BX + 1) * side] = w2 * (planes_ref[side] * value - fine)
    y_w = []
    for side, edge, near_edge in ((0, 0, 1), (1, OUT_Y - 1, OUT_Y - 2)):
        fine = jnp.broadcast_to(middle[edge : edge + 1, :], (BX, NZ))
        value = crows_ref[side] + fine + middle[near_edge : near_edge + 1, :] + zsum(fine)
        value = value + shifted_sum(fine, low[edge : edge + 1, :], high[edge : edge + 1, :])
        y_w.append(w2 * (rows_ref[side] * value - fine))
    for x in range(BX):
        around = beside + (s_low if x == 0 else s) + (s_high if x == BX - 1 else s)
        w_ref[x + 1] = w2 * (inverse_ref[x] * (c3_ref[x] + around) - s)
    copies = []
    for x in range(BX):
        w = w_ref[x + 1]
        near = w_ref[x] + w_ref[x + 2] + zsum(w)
        near = near + shifted_sum(w, y_w[0][x : x + 1, :], y_w[1][x : x + 1, :])
        out_ref[x] = base_ref[x] + s + w + w1 * ((1.0 - w2) / w2 * w + inverse_ref[x] * near)
        copies += fetch([(out_ref.at[x], out_hbm.at[x])], sems, x)
    wait(copies)


def call(kernel, outs, ins, in_specs, out_specs, scratch=(), sems=0, cost=None):
    scratch = [pltpu.VMEM(shape, F32) for shape in scratch]
    if sems:
        scratch.append(pltpu.SemaphoreType.DMA((sems,)))
    ins = [
        x if spec is SMEM else pltpu.with_memory_space_constraint(x, spec.memory_space)
        for x, spec in zip(ins, in_specs)
    ]
    return pl.pallas_call(
        kernel,
        out_shape=[spec.memory_space(shape, F32) for shape, spec in zip(outs, out_specs)],
        in_specs=in_specs,
        out_specs=out_specs,
        scratch_shapes=scratch,
        cost_estimate=cost,
        compiler_params=pltpu.CompilerParams(vmem_limit_bytes=20 * 1024 * 1024),
    )(*ins)


def body(cotangent, coefficient):
    table, into, out_table = tables()
    along_x = ("x", "y", "core")
    core = lax.axis_index("core")
    place = jnp.stack([core, lax.axis_index("x") * 4 + lax.axis_index("y"), lax.axis_index("gy")])
    place = place.astype(jnp.int32)
    near_pairs = [(i, i ^ 1) for i in range(GX)]
    far_pairs = [(i, (i + 1) % GX if i % 2 else (i - 1) % GX) for i in range(GX)]
    up = [(i, (i + 1) % GY) for i in range(GY)]
    down = [(i, (i - 1) % GY) for i in range(GY)]

    def near_swap(v):
        return lax.ppermute(v, along_x, near_pairs)

    def far_swap(v):
        return lax.ppermute(v, along_x, far_pairs)

    brick, plane, rows = (BX, BY, NZ), (BY, NZ), (BX, NZ)
    near, far, tiny_near, tiny_far, y_low, y_high, cot, coef = call(
        pack_kernel,
        [(3,) + plane, (3,) + plane, (2, NZ), (2, NZ), (24, NZ), (24, NZ), brick, brick],
        [place, cotangent, coefficient],
        [SMEM, HBM, HBM],
        [VMEM] * 8,
        sems=2 * BX,
    )
    tiny_near, tiny_far = near_swap(tiny_near), far_swap(tiny_far)
    near, far = near_swap(near), far_swap(far)
    corner_low = jnp.where(core == 0, tiny_far, tiny_near)
    corner_high = jnp.where(core == 0, tiny_near, tiny_far)
    y_low = jnp.concatenate([y_low, corner_low[0:1], corner_high[0:1]], 0)
    y_high = jnp.concatenate([y_high, corner_low[1:2], corner_high[1:2]], 0)
    from_low = lax.ppermute(y_high, "gy", up)
    from_high = lax.ppermute(y_low, "gy", down)
    w5, inverse, part = call(
        local_kernel,
        [brick, brick, brick],
        [cot, coef],
        [VMEM] * 2,
        [VMEM] * 3,
        cost=pl.CostEstimate(flops=40 * BX * BY * NZ, bytes_accessed=5 * 4 * BX * BY * NZ, transcendentals=0),
    )
    c3, base, inverse, planes, edge_rows, c_near, c_far, cy_low, cy_high, send = call(
        first_kernel,
        [brick, brick, brick, (2,) + plane, (2,) + rows, plane, plane, rows, rows, (CHIPS * GY, 4, 2 * CZ)],
        [place, w5, inverse, part, near, far, from_low, from_high, jnp.asarray(into)],
        [SMEM] + [VMEM] * 7 + [HBM],
        [HBM] * 5 + [VMEM] * 5,
        scratch=[(2,) + plane, (BX + 2,) + plane, brick, brick, (NZ, CZ)],
        sems=3 * BX + 5,
    )
    got = lax.all_to_all(send, ("x", "y", "gy"), 0, 0, tiled=True)
    c_near, c_far = near_swap(c_near), far_swap(c_far)
    c_from_low = lax.ppermute(cy_high, "gy", up)
    c_from_high = lax.ppermute(cy_low, "gy", down)
    got = got.reshape(CHIPS, ROWS, 2 * CZ)
    own, other, *rest = call(
        coarse_kernel,
        [(3 * OUT_Y, 2 * CZ)] * 2
        + [(2 * CZ, NZ), brick, brick, brick, (2,) + plane, (2,) + rows, (2,) + plane, (2,) + rows],
        [place, got, jnp.asarray(table), jnp.asarray(out_table), c3, base, inverse, planes, edge_rows]
        + [c_near, c_far, c_from_low, c_from_high],
        [SMEM, VMEM] + [HBM] * 11,
        [VMEM] * 10,
        scratch=[(CX // 2 + 1, OUT_Y + 3, GY, 2 * CZ), (CHIPS, 4, GY, 2 * CZ), (OUT_X * OUT_Y, 2 * CZ)],
        sems=CX // 2 + 1 + 3 * BX + 7,
    )
    other = near_swap(other)
    return call(
        last_kernel,
        [brick],
        [place, own, other, *rest],
        [SMEM] + [VMEM] * 10,
        [HBM],
        scratch=[(BX + 2,) + plane, brick],
        sems=BX,
    )[0]


def solution(mesh):
    split = Mesh(np.asarray(mesh.devices).reshape(4, 4, 2, GY), ("x", "y", "core", "gy"))
    spec = P(("x", "y", "core"), "gy", None)
    return jax.shard_map(body, mesh=split, in_specs=(spec, spec), out_specs=spec, check_vma=False)
```

```python
import math

import jax
import jax.numpy as jnp
import numpy as np
from jax import lax
from jax.experimental import pallas as pl
from jax.experimental.pallas import tpu as pltpu
from jax.sharding import Mesh
from jax.sharding import PartitionSpec as P

screen = 0.02
w1 = 1.0 / (1.25 + 0.75 * math.cos(math.pi / 4.0))
w2 = 1.0 / (1.25 - 0.75 * math.cos(math.pi / 4.0))

BX, BY, NZ = 8, 64, 512
CX, CY, CZ = 32, 64, 64
GX, GY = 32, 8
CHIPS = GX // 2
ROWS = CY // 2
OUT_Y = BY // 8 + 2
OUT_X = 4

VMEM = pl.BlockSpec(memory_space=pltpu.VMEM)
SMEM = pl.BlockSpec(memory_space=pltpu.SMEM)
HBM = pl.BlockSpec(memory_space=pltpu.HBM)
F32 = jnp.float32


def basis():
    place = np.arange(CZ)
    columns, freq = [], []
    for k in range(CZ // 2 + 1):
        scale = math.sqrt((1.0 if k in (0, CZ // 2) else 2.0) / CZ)
        columns.append(scale * np.cos(2.0 * math.pi * k * place / CZ))
        freq.append(k)
    for k in range(1, CZ // 2):
        columns.append(math.sqrt(2.0 / CZ) * np.sin(2.0 * math.pi * k * place / CZ))
        freq.append(k)
    return np.stack(columns, 1), np.array(freq)


def symbol(length):
    return 2.0 - 2.0 * np.cos(2.0 * math.pi * np.arange(length) / length)


def tables():
    columns, freq = basis()
    spectrum = (
        screen
        + symbol(CX)[:, None, None]
        + symbol(CY)[None, :, None]
        + symbol(CZ)[freq][None, None, :]
    )
    green = np.real(np.fft.ifft2(1.0 / spectrum, axes=(0, 1)))
    t, d, h = np.meshgrid(np.arange(OUT_Y + 3), np.arange(GY), np.arange(2), indexing="ij")
    shift = (t - 4 - 8 * d - 4 * h) % CY
    table = green[: CX // 2 + 1][:, shift].reshape(CX // 2 + 1, OUT_Y + 3, GY, 2 * CZ)
    table = table.astype(np.float32)
    into = np.repeat(columns, NZ // CZ, axis=0).astype(np.float32)
    out = np.concatenate([into.T, into.T], 0) / 8.0
    return table, into, out.astype(np.float32)


def zsum(v):
    return pltpu.roll(v, 1, 1) + pltpu.roll(v, NZ - 1, 1)


def shifted_sum(v, low, high):
    size = v.shape[0]
    row = lax.broadcasted_iota(jnp.int32, v.shape, 0)
    before = jnp.where(row == 0, low, pltpu.roll(v, 1, 0))
    after = jnp.where(row == size - 1, high, pltpu.roll(v, size - 1, 0))
    return before + after


def fetch(pairs, sems, first=0):
    copies = [pltpu.make_async_copy(s, d, sems.at[first + i]) for i, (s, d) in enumerate(pairs)]
    for copy in copies:
        copy.start()
    return copies


def wait(copies):
    for copy in copies:
        copy.wait()


def strip_kernel(core_ref, cot_ref, coef_ref, tnear_ref, tfar_ref, ylow_ref, yhigh_ref):
    core = core_ref[0]
    for side, out in ((0, ylow_ref), (1, yhigh_ref)):
        order = (0, 1, 2) if side == 0 else (7, 6, 5)
        cot = [cot_ref[side, :, r, :] for r in order]
        inverse = [1.0 / (6.0 + coef_ref[side, :, r, :]) for r in order]
        w5 = [w2 * v * i for v, i in zip(cot, inverse)]
        none = jnp.zeros((1, NZ), F32)
        kept = (1.0 - w2) * cot[0] + w5[1]
        out[0:8, :] = w5[0]
        out[8:16, :] = inverse[0]
        out[16:24, :] = kept
        c4 = (1.0 - w2) * cot[1] + w5[0] + w5[2] + zsum(w5[1]) + shifted_sum(w5[1], none, none)
        out[24:32, :] = w1 * inverse[1] * c4
        out[32:33, :] = inverse[1][0:1, :]
        out[33:34, :] = inverse[1][7:8, :]

        def corner(edge, inner):
            at = slice(edge, edge + 1)
            return w5[0][at], inverse[0][at], kept[at] + w5[0][inner : inner + 1], w5[1][at]

        for i, (low, high) in enumerate(zip(corner(0, 1), corner(BX - 1, BX - 2))):
            place = slice(4 * side + i, 4 * side + i + 1)
            tnear_ref[place, :] = jnp.where(core == 0, high, low)
            tfar_ref[place, :] = jnp.where(core == 0, low, high)


def edge_kernel(core_ref, cot_hbm, coef_hbm, near_ref, far_ref, cot_strip_ref, coef_strip_ref, cot_ref, coef_ref, sems):
    core = core_ref[0]
    pairs = []
    for hbm, ref, strip in ((cot_hbm, cot_ref, cot_strip_ref), (coef_hbm, coef_ref, coef_strip_ref)):
        pairs += [(hbm.at[pl.ds((BX - 2) * i, 2)], ref.at[pl.ds(2 * i, 2)]) for i in range(2)]
        pairs += [(hbm.at[:, pl.ds((BY - 8) * i, 8), :], strip.at[i]) for i in range(2)]
    copies = fetch(pairs, sems)
    wait(copies[0:2] + copies[4:6])
    for out, edge, step in (
        (far_ref, 3 * core, 1 - 2 * core),
        (near_ref, 3 * (1 - core), 2 * core - 1),
    ):
        cot = cot_ref[edge]
        inverse = 1.0 / (6.0 + coef_ref[edge])
        out[0] = w2 * cot * inverse
        out[1] = inverse
        out[2] = (1.0 - w2) * cot + w2 * cot_ref[edge + step] / (6.0 + coef_ref[edge + step])
    wait(copies[2:4] + copies[6:8])


def local_kernel(cot_ref, coef_ref, w5_ref, inverse_ref, c4_ref):
    for x in range(BX):
        inverse = 1.0 / (6.0 + coef_ref[x])
        inverse_ref[x] = inverse
        w5_ref[x] = w2 * cot_ref[x] * inverse
    none = jnp.zeros((1, NZ), F32)
    for x in range(BX):
        w5 = w5_ref[x]
        c4 = (1.0 - w2) * cot_ref[x] + zsum(w5) + shifted_sum(w5, none, none)
        if x > 0:
            c4 = c4 + w5_ref[x - 1]
        if x < BX - 1:
            c4 = c4 + w5_ref[x + 1]
        c4_ref[x] = c4


def first_kernel(
    core_ref, w5_ref, inverse_ref, part_ref, near_ref, far_ref, ylow_ref, yhigh_ref, into_ref,
    rows_ref, cnear_ref, cfar_ref, send_ref, c3_hbm, base_hbm, inverse_hbm, planes_hbm,
    halo_ref, w4_ref, base_ref, c3_ref, sems,
):
    core = core_ref[0]
    copies = fetch(
        [
            (inverse_ref, inverse_hbm),
            (near_ref.at[1], planes_hbm.at[1 - core]),
            (far_ref.at[1], planes_hbm.at[core]),
        ],
        sems,
    )
    for halo, side, at_high in ((near_ref, 1 - core, core == 0), (far_ref, core, core == 1)):
        halo_ref[side] = halo[0]
        low = jnp.where(at_high, ylow_ref[36:37, :], ylow_ref[32:33, :])
        high = jnp.where(at_high, yhigh_ref[36:37, :], yhigh_ref[32:33, :])
        w5 = halo[0]
        c4 = halo[2] + w5_ref[(BX - 1) * side] + zsum(w5) + shifted_sum(w5, low, high)
        w4_ref[(BX + 1) * side] = w1 * halo[1] * c4
    row = lax.broadcasted_iota(jnp.int32, (8, NZ), 0)
    for x in range(BX):
        low = jnp.where(row == 0, ylow_ref[x : x + 1, :], 0.0)
        high = jnp.where(row == 7, yhigh_ref[x : x + 1, :], 0.0)
        part = part_ref[x]
        c4 = jnp.concatenate([part[0:8, :] + low, part[8 : BY - 8, :], part[BY - 8 : BY, :] + high], 0)
        if x == 0:
            c4 = c4 + halo_ref[0]
        if x == BX - 1:
            c4 = c4 + halo_ref[1]
        w4 = w1 * inverse_ref[x] * c4
        w4_ref[x + 1] = w4
        base_ref[x] = w5_ref[x] + w4
        c3_ref[x] = c4
        copies += fetch([(base_ref.at[x], base_hbm.at[x])], sems, 3 + x)
    y4 = []
    for side, packet, edge in ((0, ylow_ref, 0), (1, yhigh_ref, BY - 1)):
        w5, corners = packet[0:8, :], packet[32:40, :]
        inverse = packet[8:16, :]
        c4 = packet[16:24, :] + w5_ref[:, edge, :] + zsum(w5)
        c4 = c4 + shifted_sum(w5, corners[0:1, :], corners[4:5, :])
        w4 = w1 * inverse * c4
        y4.append(w4)
        beside = zsum(corners)
        ends = []
        for i, at, x_side in ((0, 0, 0), (4, BX - 1, 1)):
            c4_corner = corners[i + 2 : i + 3, :] + beside[i : i + 1, :] + w5[at : at + 1, :]
            c4_corner = c4_corner + halo_ref[x_side, edge : edge + 1, :]
            ends.append(w1 * corners[i + 1 : i + 2, :] * c4_corner)
        beyond = packet[24:32, :]
        beyond = beyond + jnp.where(row == 0, w1 * packet[40:41, :] * corners[3:4, :], 0.0)
        beyond = beyond + jnp.where(row == BX - 1, w1 * packet[41:42, :] * corners[7:8, :], 0.0)
        c3 = (1.0 - w1) * c4 + beyond + w4_ref[1 : BX + 1, edge, :] + zsum(w4) + shifted_sum(w4, *ends)
        rows_ref[side] = c3
        rows_ref[2 + side] = inverse
    total = jnp.zeros((BY, NZ), F32)
    for x in range(BX):
        w4 = w4_ref[x + 1]
        c3 = (1.0 - w1) * c3_ref[x] + w4_ref[x] + w4_ref[x + 2] + zsum(w4)
        c3 = c3 + shifted_sum(w4, y4[0][x : x + 1, :], y4[1][x : x + 1, :])
        c3_ref[x] = c3
        copies += fetch([(c3_ref.at[x], c3_hbm.at[x])], sems, 3 + BX + x)
        total = total + c3
    sums = jnp.sum(total.reshape(BY // 8, 8, NZ), axis=1)
    modes = jnp.dot(sums, into_ref[...], precision=lax.Precision.HIGHEST, preferred_element_type=F32)
    packed = jnp.concatenate([modes[0:4, :], modes[4:8, :]], axis=1)
    send_ref[...] = jnp.broadcast_to(packed[None], send_ref.shape)
    cnear_ref[...] = c3_ref[(BX - 1) * (1 - core)]
    cfar_ref[...] = c3_ref[(BX - 1) * core]
    wait(copies)


def coarse_kernel(place_ref, got_ref, table_ref, own_ref, other_ref, rolled_ref):
    core, chip, gy = place_ref[0], place_ref[1], place_ref[2]
    turn = lax.rem(GY - gy, GY)
    for q in range(CHIPS):
        plane = lax.rem(chip + (1 - 2 * core) * q + CHIPS, CHIPS)
        for r in range(4):
            rolled_ref[q, r] = pltpu.roll(got_ref[plane, pl.ds(r, GY, stride=4), :], turn, 0)
    for m in range(-1, OUT_X - 1):
        at_distance = {}
        for q in range(CHIPS):
            away = (m - 2 * q) % CX
            at_distance.setdefault(min(away, CX - away), []).append(q)
        totals = [jnp.zeros((8, 2 * CZ), F32)] * OUT_Y
        for away, planes in at_distance.items():
            source = [sum(rolled_ref[q, r] for q in planes[1:]) + rolled_ref[planes[0], r] for r in range(4)]
            weight = [table_ref[away, t] for t in range(OUT_Y + 3)]
            for j in range(OUT_Y):
                for r in range(4):
                    totals[j] = totals[j] + weight[j + 3 - r] * source[r]
        for j in range(OUT_Y):
            total = jnp.sum(totals[j], axis=0, keepdims=True)
            if m < OUT_X - 2:
                at = (m + 1) * OUT_Y + j
                own_ref[at : at + 1, :] = total
            if m > -1:
                at = (OUT_X - 2 - m) * OUT_Y + j
                other_ref[at : at + 1, :] = total


def last_kernel(
    core_ref, own_ref, other_ref, out_table_ref, c3_ref, base_ref, inverse_ref, planes_ref, rows_ref, cnear_ref, cfar_ref,
    out_hbm, w_ref, out_ref, sems,
):
    core = core_ref[0]
    modes = own_ref[...] + other_ref[...]
    coarse = jnp.dot(modes, out_table_ref[...], precision=lax.Precision.HIGHEST, preferred_element_type=F32)
    outer, middle, inner = (coarse[m * OUT_Y : (m + 1) * OUT_Y, :] for m in range(3))
    low = jnp.where(core == 0, outer, inner)
    high = jnp.where(core == 0, inner, outer)

    def rows_of(plane):
        return jnp.concatenate([jnp.broadcast_to(plane[j : j + 1, :], (8, NZ)) for j in range(1, OUT_Y - 1)], 0)

    def side_sum(plane, fine):
        return shifted_sum(fine, plane[0:1, :], plane[OUT_Y - 1 : OUT_Y, :]) + zsum(fine)

    s, s_low, s_high = rows_of(middle), rows_of(low), rows_of(high)
    beside = side_sum(middle, s)
    for side, fine, plane in ((0, s_low, low), (1, s_high, high)):
        beyond = jnp.where((core == 0) == (side == 1), cnear_ref[...], cfar_ref[...])
        value = beyond + fine + s + side_sum(plane, fine)
        w_ref[(BX + 1) * side] = w2 * (planes_ref[side] * value - fine)
    y_w = []
    for side, edge, near_edge in ((0, 0, 1), (1, OUT_Y - 1, OUT_Y - 2)):
        fine = jnp.broadcast_to(middle[edge : edge + 1, :], (BX, NZ))
        value = rows_ref[side] + fine + middle[near_edge : near_edge + 1, :] + zsum(fine)
        value = value + shifted_sum(fine, low[edge : edge + 1, :], high[edge : edge + 1, :])
        y_w.append(w2 * (rows_ref[2 + side] * value - fine))
    for x in range(BX):
        around = beside + (s_low if x == 0 else s) + (s_high if x == BX - 1 else s)
        w_ref[x + 1] = w2 * (inverse_ref[x] * (c3_ref[x] + around) - s)
    copies = []
    for x in range(BX):
        w = w_ref[x + 1]
        near = w_ref[x] + w_ref[x + 2] + zsum(w)
        near = near + shifted_sum(w, y_w[0][x : x + 1, :], y_w[1][x : x + 1, :])
        out_ref[x] = base_ref[x] + s + w + w1 * ((1.0 - w2) / w2 * w + inverse_ref[x] * near)
        copies += fetch([(out_ref.at[x], out_hbm.at[x])], sems, x)
    wait(copies)


def call(kernel, outs, ins, in_specs, out_specs, scratch=(), sems=0, cost=None, aliases=None):
    scratch = [pltpu.VMEM(shape, F32) for shape in scratch]
    if sems:
        scratch.append(pltpu.SemaphoreType.DMA((sems,)))
    ins = [
        x if spec is SMEM else pltpu.with_memory_space_constraint(x, spec.memory_space)
        for x, spec in zip(ins, in_specs)
    ]
    return pl.pallas_call(
        kernel,
        out_shape=[spec.memory_space(shape, F32) for shape, spec in zip(outs, out_specs)],
        in_specs=in_specs,
        out_specs=out_specs,
        scratch_shapes=scratch,
        cost_estimate=cost,
        input_output_aliases=aliases or {},
        compiler_params=pltpu.CompilerParams(vmem_limit_bytes=12 * 1024 * 1024),
    )(*ins)


def hold_kernel(*refs):
    pass


def body(cotangent, coefficient):
    table, into, out_table = tables()
    along_x = ("x", "y", "core")
    core = lax.axis_index("core")
    place = jnp.stack([core, lax.axis_index("x") * 4 + lax.axis_index("y"), lax.axis_index("gy")])
    place = place.astype(jnp.int32)
    near_pairs = [(i, i ^ 1) for i in range(GX)]
    far_pairs = [(i, (i + 1) % GX if i % 2 else (i - 1) % GX) for i in range(GX)]
    up = [(i, (i + 1) % GY) for i in range(GY)]
    down = [(i, (i - 1) % GY) for i in range(GY)]

    def near_swap(v):
        return lax.ppermute(v, along_x, near_pairs)

    def far_swap(v):
        return lax.ppermute(v, along_x, far_pairs)

    brick, plane = (BX, BY, NZ), (BY, NZ)
    strips = (2, BX, 8, NZ)
    near, far, cot_strips, coef_strips = call(
        edge_kernel,
        [(3,) + plane, (3,) + plane, strips, strips],
        [place, cotangent, coefficient],
        [SMEM, HBM, HBM],
        [VMEM] * 4,
        scratch=[(4,) + plane, (4,) + plane],
        sems=8,
    )
    far, near = far_swap(far), near_swap(near)
    tiny_near, tiny_far, y_low, y_high = call(
        strip_kernel,
        [(8, NZ), (8, NZ), (34, NZ), (34, NZ)],
        [place, cot_strips, coef_strips],
        [SMEM, VMEM, VMEM],
        [VMEM] * 4,
        cost=pl.CostEstimate(flops=40 * BX * BY * NZ, bytes_accessed=5 * 4 * BX * BY * NZ, transcendentals=0),
    )
    tiny_near, tiny_far = near_swap(tiny_near), far_swap(tiny_far)
    corner_low = jnp.where(core == 0, tiny_far, tiny_near)
    corner_high = jnp.where(core == 0, tiny_near, tiny_far)
    y_low = jnp.concatenate([y_low[:32], corner_low[:4], corner_high[:4], y_low[32:]], 0)
    y_high = jnp.concatenate([y_high[:32], corner_low[4:], corner_high[4:], y_high[32:]], 0)
    from_low = lax.ppermute(y_high, "gy", up)
    from_high = lax.ppermute(y_low, "gy", down)
    w5, inverse, part = call(
        local_kernel,
        [brick, brick, brick],
        [cotangent, coefficient],
        [VMEM] * 2,
        [VMEM] * 3,
        cost=pl.CostEstimate(flops=40 * BX * BY * NZ, bytes_accessed=5 * 4 * BX * BY * NZ, transcendentals=0),
    )
    rows, c_near, c_far, send, c3, base, inverse, planes = call(
        first_kernel,
        [(4, BX, NZ), plane, plane, (CHIPS * GY, 4, 2 * CZ), brick, brick, brick, (2,) + plane],
        [place, w5, inverse, part, near, far, from_low, from_high, jnp.asarray(into)],
        [SMEM] + [VMEM] * 8,
        [VMEM] * 4 + [HBM] * 4,
        scratch=[(2,) + plane, (BX + 2,) + plane, brick, brick],
        sems=2 * BX + 3,
    )
    got = lax.all_to_all(send, ("x", "y", "gy"), 0, 0, tiled=True)
    c_near, c_far = near_swap(c_near), far_swap(c_far)
    table = jnp.asarray(table)
    got, c3, base, inverse, planes = call(
        hold_kernel,
        [got.shape, brick, brick, brick, (2,) + plane],
        [got, c3, base, inverse, planes, table],
        [VMEM] + [HBM] * 4 + [VMEM],
        [VMEM] + [HBM] * 4,
        aliases={i: i for i in range(5)},
    )
    own, other = call(
        coarse_kernel,
        [(3 * OUT_Y, 2 * CZ)] * 2,
        [place, got.reshape(CHIPS, ROWS, 2 * CZ), table],
        [SMEM, VMEM, VMEM],
        [VMEM] * 2,
        scratch=[(CHIPS, 4, GY, 2 * CZ)],
        cost=pl.CostEstimate(flops=10**11, bytes_accessed=10**7, transcendentals=0),
    )
    other = near_swap(other)
    return call(
        last_kernel,
        [brick],
        [place, own, other, jnp.asarray(out_table), c3, base, inverse, planes, rows, c_near, c_far],
        [SMEM] + [VMEM] * 10,
        [HBM],
        scratch=[(BX + 2,) + plane, brick],
        sems=BX,
    )[0]


def solution(mesh):
    split = Mesh(np.asarray(mesh.devices).reshape(4, 4, 2, GY), ("x", "y", "core", "gy"))
    spec = P(("x", "y", "core"), "gy", None)
    return jax.shard_map(body, mesh=split, in_specs=(spec, spec), out_specs=spec, check_vma=False)
```

```python
import math

import jax
import jax.numpy as jnp
import numpy as np
from jax import lax
from jax.experimental import pallas as pl
from jax.experimental.pallas import tpu as pltpu
from jax.sharding import Mesh
from jax.sharding import PartitionSpec as P

screen = 0.02
w1 = 1.0 / (1.25 + 0.75 * math.cos(math.pi / 4.0))
w2 = 1.0 / (1.25 - 0.75 * math.cos(math.pi / 4.0))

BX, BY, NZ = 8, 64, 512
CX, CY, CZ = 32, 64, 64
GX, GY = 32, 8
MATES = 4
GROUPS = GX // MATES
ROWS = CY // 2
OUT_Y = BY // 8 + 2
OUT_X = MATES + 2

VMEM = pl.BlockSpec(memory_space=pltpu.VMEM)
SMEM = pl.BlockSpec(memory_space=pltpu.SMEM)
HBM = pl.BlockSpec(memory_space=pltpu.HBM)
F32 = jnp.float32


def basis():
    place = np.arange(CZ)
    columns, freq = [], []
    for k in range(CZ // 2 + 1):
        scale = math.sqrt((1.0 if k in (0, CZ // 2) else 2.0) / CZ)
        columns.append(scale * np.cos(2.0 * math.pi * k * place / CZ))
        freq.append(k)
    for k in range(1, CZ // 2):
        columns.append(math.sqrt(2.0 / CZ) * np.sin(2.0 * math.pi * k * place / CZ))
        freq.append(k)
    return np.stack(columns, 1), np.array(freq)


def symbol(length):
    return 2.0 - 2.0 * np.cos(2.0 * math.pi * np.arange(length) / length)


def tables():
    columns, freq = basis()
    spectrum = (
        screen
        + symbol(CX)[:, None, None]
        + symbol(CY)[None, :, None]
        + symbol(CZ)[freq][None, None, :]
    )
    green = np.real(np.fft.ifft2(1.0 / spectrum, axes=(0, 1)))
    t, d, h = np.meshgrid(np.arange(OUT_Y + 3), np.arange(GY), np.arange(2), indexing="ij")
    shift = (t - 4 - 8 * d - 4 * h) % CY
    table = green[: CX // 2 + 1][:, shift].reshape(CX // 2 + 1, OUT_Y + 3, GY, 2 * CZ)
    table = table.astype(np.float32)
    into = np.repeat(columns, NZ // CZ, axis=0).astype(np.float32)
    out = np.concatenate([into.T, into.T], 0) / 8.0
    return table, into, out.astype(np.float32)


def zsum(v):
    return pltpu.roll(v, 1, 1) + pltpu.roll(v, NZ - 1, 1)


def shifted_sum(v, low, high):
    size = v.shape[0]
    row = lax.broadcasted_iota(jnp.int32, v.shape, 0)
    before = jnp.where(row == 0, low, pltpu.roll(v, 1, 0))
    after = jnp.where(row == size - 1, high, pltpu.roll(v, size - 1, 0))
    return before + after


def fetch(pairs, sems, first=0):
    copies = [pltpu.make_async_copy(s, d, sems.at[first + i]) for i, (s, d) in enumerate(pairs)]
    for copy in copies:
        copy.start()
    return copies


def wait(copies):
    for copy in copies:
        copy.wait()


def strip_kernel(core_ref, cot_hbm, coef_hbm, tnear_ref, tfar_ref, ylow_ref, yhigh_ref, cot_ref, coef_ref, sems):
    core = core_ref[0]
    ends = (pl.ds(0, 8), pl.ds(BY - 8, 8))
    wait(
        fetch(
            [(hbm.at[:, ends[i], :], ref.at[i]) for i in range(2) for hbm, ref in ((cot_hbm, cot_ref), (coef_hbm, coef_ref))],
            sems,
        )
    )
    for side, out in ((0, ylow_ref), (1, yhigh_ref)):
        order = (0, 1, 2) if side == 0 else (7, 6, 5)
        cot = [cot_ref[side, :, r, :] for r in order]
        inverse = [1.0 / (6.0 + coef_ref[side, :, r, :]) for r in order]
        w5 = [w2 * v * i for v, i in zip(cot, inverse)]
        none = jnp.zeros((1, NZ), F32)
        kept = (1.0 - w2) * cot[0] + w5[1]
        out[0:8, :] = w5[0]
        out[8:16, :] = inverse[0]
        out[16:24, :] = kept
        c4 = (1.0 - w2) * cot[1] + w5[0] + w5[2] + zsum(w5[1]) + shifted_sum(w5[1], none, none)
        out[24:32, :] = w1 * inverse[1] * c4
        out[32:33, :] = inverse[1][0:1, :]
        out[33:34, :] = inverse[1][7:8, :]

        def corner(edge, inner):
            at = slice(edge, edge + 1)
            return w5[0][at], inverse[0][at], kept[at] + w5[0][inner : inner + 1], w5[1][at]

        for i, (low, high) in enumerate(zip(corner(0, 1), corner(BX - 1, BX - 2))):
            place = slice(4 * side + i, 4 * side + i + 1)
            tnear_ref[place, :] = jnp.where(core == 0, high, low)
            tfar_ref[place, :] = jnp.where(core == 0, low, high)


def edge_kernel(core_ref, cot_ref, coef_ref, after_ref, near_ref, far_ref):
    core = core_ref[0]
    for out, edge, step in (
        (far_ref, (BX - 1) * core, 1 - 2 * core),
        (near_ref, (BX - 1) * (1 - core), 2 * core - 1),
    ):
        cot = cot_ref[edge]
        inverse = 1.0 / (6.0 + coef_ref[edge])
        out[0] = w2 * cot * inverse
        out[1] = inverse
        out[2] = (1.0 - w2) * cot + w2 * cot_ref[edge + step] / (6.0 + coef_ref[edge + step])


def local_kernel(
    cot_ref, coef_ref,
    w5_edges_ref, inverse_edges_ref, c3_edges_ref, rows_ref, sums_ref, c3_ref, base_hbm, inverse_hbm,
    w5_ref, inverse_ref, w4_ref, base_ref, sems,
):
    none = jnp.zeros((1, NZ), F32)
    for x in range(BX):
        inverse = 1.0 / (6.0 + coef_ref[x])
        inverse_ref[x] = inverse
        w5_ref[x] = w2 * cot_ref[x] * inverse
    copies = fetch([(inverse_ref, inverse_hbm)], sems)
    for x in range(BX):
        w5 = w5_ref[x]
        c4 = (1.0 - w2) * cot_ref[x] + zsum(w5) + shifted_sum(w5, none, none)
        if x > 0:
            c4 = c4 + w5_ref[x - 1]
        if x < BX - 1:
            c4 = c4 + w5_ref[x + 1]
        w4 = w1 * inverse_ref[x] * c4
        w4_ref[x] = w4
        base_ref[x] = w5 + w4
        c3_ref[x] = (1.0 - w1) * c4
    copies += fetch([(base_ref, base_hbm)], sems, 1)
    total = jnp.zeros((BY, NZ), F32)
    for x in range(BX):
        w4 = w4_ref[x]
        c3 = c3_ref[x] + zsum(w4) + shifted_sum(w4, none, none)
        if x > 0:
            c3 = c3 + w4_ref[x - 1]
        if x < BX - 1:
            c3 = c3 + w4_ref[x + 1]
        c3_ref[x] = c3
        total = total + c3
    sums_ref[...] = jnp.sum(total.reshape(BY // 8, 8, NZ), axis=1)
    for side, x, y in ((0, 0, 0), (1, BX - 1, BY - 1)):
        w5_edges_ref[side] = w5_ref[x]
        inverse_edges_ref[side] = inverse_ref[x]
        c3_edges_ref[side] = c3_ref[x]
        rows_ref[side] = w5_ref[:, y, :]
        rows_ref[2 + side] = inverse_ref[:, y, :]
        rows_ref[4 + side] = w4_ref[:, y, :]
    wait(copies)


def with_ends(plane, row, ends):
    low = jnp.where(row == 0, ends[0], jnp.where(row == 1, ends[1], 0.0))
    high = jnp.where(row == 6, ends[2], jnp.where(row == 7, ends[3], 0.0))
    return jnp.concatenate([plane[0:8, :] + low, plane[8 : BY - 8, :], plane[BY - 8 : BY, :] + high], 0)


def first_kernel(
    core_ref, w5_edges_ref, inverse_edges_ref, c3_edges_ref, own_rows_ref, part_sums_ref,
    near_ref, far_ref, ylow_ref, yhigh_ref, into_ref,
    rows_ref, cnear_ref, cfar_ref, send_ref, added_ref, planes_hbm,
    sems,
):
    core = core_ref[0]
    copies = fetch(
        [
            (near_ref.at[1], planes_hbm.at[1 - core]),
            (far_ref.at[1], planes_hbm.at[core]),
        ],
        sems,
    )
    none = jnp.zeros((1, NZ), F32)
    row = lax.broadcasted_iota(jnp.int32, (8, NZ), 0)
    plane_total = jnp.zeros((BY, NZ), F32)
    for halo, side, at_high in ((near_ref, 1 - core, core == 0), (far_ref, core, core == 1)):
        low = jnp.where(at_high, ylow_ref[36:37, :], ylow_ref[32:33, :])
        high = jnp.where(at_high, yhigh_ref[36:37, :], yhigh_ref[32:33, :])
        w5 = halo[0]
        c4 = halo[2] + w5_edges_ref[side] + zsum(w5) + shifted_sum(w5, low, high)
        w4_added = w1 * inverse_edges_ref[side] * w5
        c3_added = (1.0 - w1) * w5 + w1 * halo[1] * c4 + zsum(w4_added) + shifted_sum(w4_added, none, none)
        added_ref[side, 0] = c3_added
        added_ref[side, 1] = w4_added
        plane_total = plane_total + c3_added + w4_added
    sums = part_sums_ref[...] + jnp.sum(plane_total.reshape(BY // 8, 8, NZ), axis=1)
    for side, packet, edge in ((0, ylow_ref, 0), (1, yhigh_ref, BY - 1)):
        w5, corners, inverse = packet[0:8, :], packet[32:40, :], packet[8:16, :]
        c4 = packet[16:24, :] + own_rows_ref[side] + zsum(w5)
        c4 = c4 + shifted_sum(w5, corners[0:1, :], corners[4:5, :])
        w4 = w1 * inverse * c4
        w4_added = w1 * own_rows_ref[2 + side] * w5
        c3_added = (1.0 - w1) * w5 + w4 + zsum(w4_added) + shifted_sum(w4_added, none, none)
        beside = zsum(corners)
        ends = []
        inner = own_rows_ref[4 + side] + w4_added
        beyond = packet[24:32, :]
        for i, at, x_side in ((0, 0, 0), (4, BX - 1, 1)):
            halo = jnp.where(
                (core == 0) == (x_side == 0), far_ref[0, edge : edge + 1, :], near_ref[0, edge : edge + 1, :]
            )
            c4_corner = corners[i + 2 : i + 3, :] + beside[i : i + 1, :] + w5[at : at + 1, :] + halo
            ends.append(w1 * corners[i + 1 : i + 2, :] * c4_corner)
            missing = w1 * packet[40 + x_side : 41 + x_side, :] * corners[i + 3 : i + 4, :]
            missing = missing + added_ref[x_side, 1, edge : edge + 1, :]
            beyond = beyond + jnp.where(row == at, missing, 0.0)
        rows_ref[side] = (1.0 - w1) * c4 + beyond + inner + zsum(w4) + shifted_sum(w4, *ends)
        rows_ref[2 + side] = inverse
        rows_ref[4 + side] = c3_added
        rows_ref[6 + side] = w4_added
        more = jnp.sum(c3_added + w4_added, axis=0, keepdims=True)
        sums = sums + jnp.where(row == 7 * side, more, 0.0)
    modes = jnp.dot(sums, into_ref[...], precision=lax.Precision.HIGHEST, preferred_element_type=F32)
    packed = jnp.concatenate([modes[0:4, :], modes[4:8, :]], axis=1)
    send_ref[...] = jnp.broadcast_to(packed[None], send_ref.shape)
    edges = []
    for side, x in ((0, 0), (1, BX - 1)):
        at = slice(x, x + 1)
        ends = (rows_ref[4, at, :], rows_ref[6, at, :], rows_ref[7, at, :], rows_ref[5, at, :])
        edges.append(with_ends(c3_edges_ref[side] + added_ref[side, 0], row, ends))
    cnear_ref[...] = jnp.where(core == 0, edges[1], edges[0])
    cfar_ref[...] = jnp.where(core == 0, edges[0], edges[1])
    wait(copies)


def coarse_kernel(place_ref, got_ref, table_ref, own_ref, one_ref, two_ref, three_ref, rolled_ref, sums_ref):
    mate, group, gy = place_ref[1], place_ref[2], place_ref[3]
    turn = lax.rem(GY - gy, GY)
    for q in range(GROUPS):
        plane = lax.rem(group + q, GROUPS)
        for r in range(4):
            rolled_ref[q, r] = pltpu.roll(got_ref[plane, pl.ds(r, GY, stride=4), :], turn, 0)
    for m in range(OUT_X):
        totals = [jnp.zeros((8, 2 * CZ), F32)] * OUT_Y
        for q in range(GROUPS):
            away = jnp.abs(m - 1 - mate - MATES * q)
            away = jnp.minimum(away, jnp.abs(CX - away))
            source = [rolled_ref[q, r] for r in range(4)]
            weight = [table_ref[away, t] for t in range(OUT_Y + 3)]
            for j in range(OUT_Y):
                for r in range(4):
                    totals[j] = totals[j] + weight[j + 3 - r] * source[r]
        for j in range(OUT_Y):
            sums_ref[m, j : j + 1, :] = jnp.sum(totals[j], axis=0, keepdims=True)
    for flip, out in enumerate((own_ref, one_ref, two_ref, three_ref)):
        first = lax.bitwise_xor(mate, flip)
        for m in range(3):
            out[m * OUT_Y : (m + 1) * OUT_Y, :] = sums_ref[first + m]


def last_kernel(
    core_ref, own_ref, one_ref, two_ref, three_ref, out_table_ref, c3_ref, base_ref, inverse_ref, planes_ref, added_ref, rows_ref, cnear_ref, cfar_ref,
    out_hbm, w_ref, out_ref, sems,
):
    core = core_ref[0]
    modes = (own_ref[...] + one_ref[...]) + (two_ref[...] + three_ref[...])
    coarse = jnp.dot(modes, out_table_ref[...], precision=lax.Precision.HIGHEST, preferred_element_type=F32)
    low, middle, high = (coarse[m * OUT_Y : (m + 1) * OUT_Y, :] for m in range(3))

    def rows_of(plane):
        return jnp.concatenate([jnp.broadcast_to(plane[j : j + 1, :], (8, NZ)) for j in range(1, OUT_Y - 1)], 0)

    def side_sum(plane, fine):
        return shifted_sum(fine, plane[0:1, :], plane[OUT_Y - 1 : OUT_Y, :]) + zsum(fine)

    s, s_low, s_high = rows_of(middle), rows_of(low), rows_of(high)
    beside = side_sum(middle, s)
    row = lax.broadcasted_iota(jnp.int32, (8, NZ), 0)
    none = jnp.zeros((1, NZ), F32)
    added_at = {0: (0, 0), 1: (0, 1), BX - 2: (1, 1), BX - 1: (1, 0)}
    for side, fine, plane in ((0, s_low, low), (1, s_high, high)):
        beyond = jnp.where((core == 0) == (side == 1), cnear_ref[...], cfar_ref[...])
        value = beyond + fine + s + side_sum(plane, fine)
        w_ref[(BX + 1) * side] = w2 * (planes_ref[side] * value - fine)
    y_w = []
    for side, edge, near_edge in ((0, 0, 1), (1, OUT_Y - 1, OUT_Y - 2)):
        fine = jnp.broadcast_to(middle[edge : edge + 1, :], (BX, NZ))
        value = rows_ref[side] + fine + middle[near_edge : near_edge + 1, :] + zsum(fine)
        value = value + shifted_sum(fine, low[edge : edge + 1, :], high[edge : edge + 1, :])
        y_w.append(w2 * (rows_ref[2 + side] * value - fine))
    for x in range(BX):
        around = beside + (s_low if x == 0 else s) + (s_high if x == BX - 1 else s)
        at = slice(x, x + 1)
        ends = (rows_ref[4, at, :], rows_ref[6, at, :], rows_ref[7, at, :], rows_ref[5, at, :])
        c3 = with_ends(c3_ref[x], row, ends)
        if x in added_at:
            c3 = c3 + added_ref[added_at[x]]
        w_ref[x + 1] = w2 * (inverse_ref[x] * (c3 + around) - s)
    copies = []
    for x in range(BX):
        w = w_ref[x + 1]
        near = w_ref[x] + w_ref[x + 2] + zsum(w)
        near = near + shifted_sum(w, y_w[0][x : x + 1, :], y_w[1][x : x + 1, :])
        base = with_ends(base_ref[x], row, (rows_ref[6, x : x + 1, :], none, none, rows_ref[7, x : x + 1, :]))
        if x in (0, BX - 1):
            base = base + added_ref[0 if x == 0 else 1, 1]
        out_ref[x] = base + s + w + w1 * ((1.0 - w2) / w2 * w + inverse_ref[x] * near)
        copies += fetch([(out_ref.at[x], out_hbm.at[x])], sems, x)
    wait(copies)


def call(kernel, outs, ins, in_specs, out_specs, scratch=(), sems=0, cost=None, aliases=None):
    scratch = [pltpu.VMEM(shape, F32) for shape in scratch]
    if sems:
        scratch.append(pltpu.SemaphoreType.DMA((sems,)))
    ins = [
        x if spec is SMEM else pltpu.with_memory_space_constraint(x, spec.memory_space)
        for x, spec in zip(ins, in_specs)
    ]
    return pl.pallas_call(
        kernel,
        out_shape=[spec.memory_space(shape, F32) for shape, spec in zip(outs, out_specs)],
        in_specs=in_specs,
        out_specs=out_specs,
        scratch_shapes=scratch,
        cost_estimate=cost,
        input_output_aliases=aliases or {},
        compiler_params=pltpu.CompilerParams(vmem_limit_bytes=12 * 1024 * 1024),
    )(*ins)


def hold_kernel(*refs):
    pass


def body(cotangent, coefficient):
    table, into, out_table = tables()
    along_x = ("x", "pair", "chip", "core")
    core = lax.axis_index("core")
    mate = lax.axis_index("chip") * 2 + core
    place = jnp.stack([core, mate, lax.axis_index("x") * 2 + lax.axis_index("pair"), lax.axis_index("gy")])
    place = place.astype(jnp.int32)
    near_pairs = [(i, i ^ 1) for i in range(GX)]
    far_pairs = [(i, (i + 1) % GX if i % 2 else (i - 1) % GX) for i in range(GX)]
    up = [(i, (i + 1) % GY) for i in range(GY)]
    down = [(i, (i - 1) % GY) for i in range(GY)]

    def near_swap(v):
        return lax.ppermute(v, along_x, near_pairs)

    def far_swap(v):
        return lax.ppermute(v, along_x, far_pairs)

    brick, plane = (BX, BY, NZ), (BY, NZ)
    tiny_near, tiny_far, y_low, y_high = call(
        strip_kernel,
        [(8, NZ), (8, NZ), (34, NZ), (34, NZ)],
        [place, cotangent, coefficient],
        [SMEM, HBM, HBM],
        [VMEM] * 4,
        scratch=[(2, BX, 8, NZ), (2, BX, 8, NZ)],
        sems=4,
    )
    near, far = call(
        edge_kernel,
        [(3,) + plane, (3,) + plane],
        [place, cotangent, coefficient, y_low],
        [SMEM, VMEM, VMEM, VMEM],
        [VMEM] * 2,
    )
    tiny_far, tiny_near = far_swap(tiny_far), near_swap(tiny_near)
    far, near = far_swap(far), near_swap(near)
    corner_low = jnp.where(core == 0, tiny_far, tiny_near)
    corner_high = jnp.where(core == 0, tiny_near, tiny_far)
    y_low = jnp.concatenate([y_low[:32], corner_low[:4], corner_high[:4], y_low[32:]], 0)
    y_high = jnp.concatenate([y_high[:32], corner_low[4:], corner_high[4:], y_high[32:]], 0)
    from_low = lax.ppermute(y_high, "gy", up)
    from_high = lax.ppermute(y_low, "gy", down)
    edge_planes = (2,) + plane
    w5_edges, inverse_edges, c3_edges, own_rows, sums, c3, base, inverse = call(
        local_kernel,
        [edge_planes, edge_planes, edge_planes, (6, BX, NZ), (8, NZ), brick, brick, brick],
        [cotangent, coefficient],
        [VMEM] * 2,
        [VMEM] * 6 + [HBM] * 2,
        scratch=[brick] * 4,
        sems=2,
        cost=pl.CostEstimate(flops=40 * BX * BY * NZ, bytes_accessed=5 * 4 * BX * BY * NZ, transcendentals=0),
    )
    rows, c_near, c_far, send, added, planes = call(
        first_kernel,
        [(8, BX, NZ), plane, plane, (GROUPS * GY, 4, 2 * CZ), (2,) + edge_planes, edge_planes],
        [place, w5_edges, inverse_edges, c3_edges, own_rows, sums, near, far, from_low, from_high, jnp.asarray(into)],
        [SMEM] + [VMEM] * 10,
        [VMEM] * 5 + [HBM],
        sems=2,
    )
    got = lax.all_to_all(send, ("x", "pair", "gy"), 0, 0, tiled=True)
    c_near, c_far = near_swap(c_near), far_swap(c_far)
    table = jnp.asarray(table)
    got, c3, base, inverse, planes = call(
        hold_kernel,
        [got.shape, brick, brick, brick, edge_planes],
        [got, c3, base, inverse, planes, table],
        [VMEM] + [HBM] * 4 + [VMEM],
        [VMEM] + [HBM] * 4,
        aliases={i: i for i in range(5)},
    )
    own, one, two, three = call(
        coarse_kernel,
        [(3 * OUT_Y, 2 * CZ)] * 4,
        [place, got.reshape(GROUPS, ROWS, 2 * CZ), table],
        [SMEM, VMEM, VMEM],
        [VMEM] * 4,
        scratch=[(GROUPS, 4, GY, 2 * CZ), (OUT_X, OUT_Y, 2 * CZ)],
        cost=pl.CostEstimate(flops=10**11, bytes_accessed=10**7, transcendentals=0),
    )
    one, two, three = (
        lax.ppermute(v, along_x, [(i, i ^ flip) for i in range(GX)]) for flip, v in ((1, one), (2, two), (3, three))
    )
    return call(
        last_kernel,
        [brick],
        [place, own, one, two, three, jnp.asarray(out_table), c3, base, inverse, planes, added, rows, c_near, c_far],
        [SMEM] + [VMEM] * 13,
        [HBM],
        scratch=[(BX + 2,) + plane, brick],
        sems=BX,
    )[0]


def solution(mesh):
    split = Mesh(np.asarray(mesh.devices).reshape(4, 2, 2, 2, GY), ("x", "pair", "chip", "core", "gy"))
    spec = P(("x", "pair", "chip", "core"), "gy", None)
    return jax.shard_map(body, mesh=split, in_specs=(spec, spec), out_specs=spec, check_vma=False)
```

```python
import math

import jax
import jax.numpy as jnp
import numpy as np
from jax import lax
from jax.experimental import pallas as pl
from jax.experimental.pallas import tpu as pltpu
from jax.sharding import Mesh
from jax.sharding import PartitionSpec as P

screen = 0.02
w1 = 1.0 / (1.25 + 0.75 * math.cos(math.pi / 4.0))
w2 = 1.0 / (1.25 - 0.75 * math.cos(math.pi / 4.0))

BX, BY, NZ = 8, 64, 512
CX, CY, CZ = 32, 64, 64
GX, GY = 32, 8
MATES = 4
GROUPS = GX // MATES
ROWS = CY // 2
OUT_Y = BY // 8 + 2
OUT_X = MATES + 2

VMEM = pl.BlockSpec(memory_space=pltpu.VMEM)
SMEM = pl.BlockSpec(memory_space=pltpu.SMEM)
HBM = pl.BlockSpec(memory_space=pltpu.HBM)
F32 = jnp.float32


def basis():
    place = np.arange(CZ)
    columns, freq = [], []
    for k in range(CZ // 2 + 1):
        scale = math.sqrt((1.0 if k in (0, CZ // 2) else 2.0) / CZ)
        columns.append(scale * np.cos(2.0 * math.pi * k * place / CZ))
        freq.append(k)
    for k in range(1, CZ // 2):
        columns.append(math.sqrt(2.0 / CZ) * np.sin(2.0 * math.pi * k * place / CZ))
        freq.append(k)
    return np.stack(columns, 1), np.array(freq)


def symbol(length):
    return 2.0 - 2.0 * np.cos(2.0 * math.pi * np.arange(length) / length)


def tables():
    columns, freq = basis()
    spectrum = (
        screen
        + symbol(CX)[:, None, None]
        + symbol(CY)[None, :, None]
        + symbol(CZ)[freq][None, None, :]
    )
    green = np.real(np.fft.ifft2(1.0 / spectrum, axes=(0, 1)))
    t, d, h = np.meshgrid(np.arange(OUT_Y + 3), np.arange(GY), np.arange(2), indexing="ij")
    shift = (t - 4 - 8 * d - 4 * h) % CY
    table = green[: CX // 2 + 1][:, shift].reshape(CX // 2 + 1, OUT_Y + 3, GY, 2 * CZ)
    table = table.astype(np.float32)
    into = np.repeat(columns, NZ // CZ, axis=0).astype(np.float32)
    out = np.concatenate([into.T, into.T], 0) / 8.0
    return table, into, out.astype(np.float32)


def zsum(v):
    return pltpu.roll(v, 1, 1) + pltpu.roll(v, NZ - 1, 1)


def shifted_sum(v, low, high):
    size = v.shape[0]
    row = lax.broadcasted_iota(jnp.int32, v.shape, 0)
    before = jnp.where(row == 0, low, pltpu.roll(v, 1, 0))
    after = jnp.where(row == size - 1, high, pltpu.roll(v, size - 1, 0))
    return before + after


def fetch(pairs, sems, first=0):
    copies = [pltpu.make_async_copy(s, d, sems.at[first + i]) for i, (s, d) in enumerate(pairs)]
    for copy in copies:
        copy.start()
    return copies


def wait(copies):
    for copy in copies:
        copy.wait()


def strip_kernel(core_ref, cot_hbm, coef_hbm, tnear_ref, tfar_ref, ylow_ref, yhigh_ref, cot_ref, coef_ref, sems):
    core = core_ref[0]
    ends = (pl.ds(0, 8), pl.ds(BY - 8, 8))
    wait(
        fetch(
            [(hbm.at[:, ends[i], :], ref.at[i]) for i in range(2) for hbm, ref in ((cot_hbm, cot_ref), (coef_hbm, coef_ref))],
            sems,
        )
    )
    for side, out in ((0, ylow_ref), (1, yhigh_ref)):
        order = (0, 1, 2) if side == 0 else (7, 6, 5)
        cot = [cot_ref[side, :, r, :] for r in order]
        inverse = [1.0 / (6.0 + coef_ref[side, :, r, :]) for r in order]
        w5 = [w2 * v * i for v, i in zip(cot, inverse)]
        none = jnp.zeros((1, NZ), F32)
        kept = (1.0 - w2) * cot[0] + w5[1]
        out[0:8, :] = w5[0]
        out[8:16, :] = inverse[0]
        out[16:24, :] = kept
        c4 = (1.0 - w2) * cot[1] + w5[0] + w5[2] + zsum(w5[1]) + shifted_sum(w5[1], none, none)
        out[24:32, :] = w1 * inverse[1] * c4
        out[32:33, :] = inverse[1][0:1, :]
        out[33:34, :] = inverse[1][7:8, :]

        def corner(edge, inner):
            at = slice(edge, edge + 1)
            return w5[0][at], inverse[0][at], kept[at] + w5[0][inner : inner + 1], w5[1][at]

        for i, (low, high) in enumerate(zip(corner(0, 1), corner(BX - 1, BX - 2))):
            place = slice(4 * side + i, 4 * side + i + 1)
            tnear_ref[place, :] = jnp.where(core == 0, high, low)
            tfar_ref[place, :] = jnp.where(core == 0, low, high)


def edge_kernel(core_ref, cot_ref, coef_ref, after_ref, near_ref, far_ref):
    core = core_ref[0]
    for out, edge, step in (
        (far_ref, (BX - 1) * core, 1 - 2 * core),
        (near_ref, (BX - 1) * (1 - core), 2 * core - 1),
    ):
        cot = cot_ref[edge]
        inverse = 1.0 / (6.0 + coef_ref[edge])
        out[0] = w2 * cot * inverse
        out[1] = inverse
        out[2] = (1.0 - w2) * cot + w2 * cot_ref[edge + step] / (6.0 + coef_ref[edge + step])


def local_kernel(
    cot_ref, coef_ref,
    w5_edges_ref, inverse_edges_ref, c3_edges_ref, rows_ref, sums_ref, c3_ref, base_hbm, inverse_hbm,
    w5_ref, inverse_ref, w4_ref, base_ref, sems,
):
    none = jnp.zeros((1, NZ), F32)
    for x in range(BX):
        inverse = 1.0 / (6.0 + coef_ref[x])
        inverse_ref[x] = inverse
        w5_ref[x] = w2 * cot_ref[x] * inverse
    copies = fetch([(inverse_ref, inverse_hbm)], sems)
    for x in range(BX):
        w5 = w5_ref[x]
        c4 = (1.0 - w2) * cot_ref[x] + zsum(w5) + shifted_sum(w5, none, none)
        if x > 0:
            c4 = c4 + w5_ref[x - 1]
        if x < BX - 1:
            c4 = c4 + w5_ref[x + 1]
        w4 = w1 * inverse_ref[x] * c4
        w4_ref[x] = w4
        base_ref[x] = w5 + w4
        c3_ref[x] = (1.0 - w1) * c4
    copies += fetch([(base_ref, base_hbm)], sems, 1)
    total = jnp.zeros((BY, NZ), F32)
    for x in range(BX):
        w4 = w4_ref[x]
        c3 = c3_ref[x] + zsum(w4) + shifted_sum(w4, none, none)
        if x > 0:
            c3 = c3 + w4_ref[x - 1]
        if x < BX - 1:
            c3 = c3 + w4_ref[x + 1]
        c3_ref[x] = c3
        total = total + c3
    sums_ref[...] = jnp.sum(total.reshape(BY // 8, 8, NZ), axis=1)
    for side, x, y in ((0, 0, 0), (1, BX - 1, BY - 1)):
        w5_edges_ref[side] = w5_ref[x]
        inverse_edges_ref[side] = inverse_ref[x]
        c3_edges_ref[side] = c3_ref[x]
        rows_ref[side] = w5_ref[:, y, :]
        rows_ref[2 + side] = inverse_ref[:, y, :]
        rows_ref[4 + side] = w4_ref[:, y, :]
    wait(copies)


def with_ends(plane, row, ends):
    low = jnp.where(row == 0, ends[0], jnp.where(row == 1, ends[1], 0.0))
    high = jnp.where(row == 6, ends[2], jnp.where(row == 7, ends[3], 0.0))
    return jnp.concatenate([plane[0:8, :] + low, plane[8 : BY - 8, :], plane[BY - 8 : BY, :] + high], 0)


def first_kernel(
    core_ref, w5_edges_ref, inverse_edges_ref, c3_edges_ref, own_rows_ref, part_sums_ref, c3_ref,
    near_ref, far_ref, ylow_ref, yhigh_ref, into_ref,
    rows_ref, cnear_ref, cfar_ref, added_ref, send_hbm, planes_hbm, c3_hbm,
    send_ref, sems,
):
    core = core_ref[0]
    copies = fetch(
        [
            (c3_ref, c3_hbm),
            (near_ref.at[1], planes_hbm.at[1 - core]),
            (far_ref.at[1], planes_hbm.at[core]),
        ],
        sems,
    )
    none = jnp.zeros((1, NZ), F32)
    row = lax.broadcasted_iota(jnp.int32, (8, NZ), 0)
    plane_total = jnp.zeros((BY, NZ), F32)
    for halo, side, at_high in ((near_ref, 1 - core, core == 0), (far_ref, core, core == 1)):
        low = jnp.where(at_high, ylow_ref[36:37, :], ylow_ref[32:33, :])
        high = jnp.where(at_high, yhigh_ref[36:37, :], yhigh_ref[32:33, :])
        w5 = halo[0]
        c4 = halo[2] + w5_edges_ref[side] + zsum(w5) + shifted_sum(w5, low, high)
        w4_added = w1 * inverse_edges_ref[side] * w5
        c3_added = (1.0 - w1) * w5 + w1 * halo[1] * c4 + zsum(w4_added) + shifted_sum(w4_added, none, none)
        added_ref[side, 0] = c3_added
        added_ref[side, 1] = w4_added
        plane_total = plane_total + c3_added + w4_added
    sums = part_sums_ref[...] + jnp.sum(plane_total.reshape(BY // 8, 8, NZ), axis=1)
    for side, packet, edge in ((0, ylow_ref, 0), (1, yhigh_ref, BY - 1)):
        w5, corners, inverse = packet[0:8, :], packet[32:40, :], packet[8:16, :]
        c4 = packet[16:24, :] + own_rows_ref[side] + zsum(w5)
        c4 = c4 + shifted_sum(w5, corners[0:1, :], corners[4:5, :])
        w4 = w1 * inverse * c4
        w4_added = w1 * own_rows_ref[2 + side] * w5
        c3_added = (1.0 - w1) * w5 + w4 + zsum(w4_added) + shifted_sum(w4_added, none, none)
        beside = zsum(corners)
        ends = []
        inner = own_rows_ref[4 + side] + w4_added
        beyond = packet[24:32, :]
        for i, at, x_side in ((0, 0, 0), (4, BX - 1, 1)):
            halo = jnp.where(
                (core == 0) == (x_side == 0), far_ref[0, edge : edge + 1, :], near_ref[0, edge : edge + 1, :]
            )
            c4_corner = corners[i + 2 : i + 3, :] + beside[i : i + 1, :] + w5[at : at + 1, :] + halo
            ends.append(w1 * corners[i + 1 : i + 2, :] * c4_corner)
            missing = w1 * packet[40 + x_side : 41 + x_side, :] * corners[i + 3 : i + 4, :]
            missing = missing + added_ref[x_side, 1, edge : edge + 1, :]
            beyond = beyond + jnp.where(row == at, missing, 0.0)
        rows_ref[side] = (1.0 - w1) * c4 + beyond + inner + zsum(w4) + shifted_sum(w4, *ends)
        rows_ref[2 + side] = inverse
        rows_ref[4 + side] = c3_added
        rows_ref[6 + side] = w4_added
        more = jnp.sum(c3_added + w4_added, axis=0, keepdims=True)
        sums = sums + jnp.where(row == 7 * side, more, 0.0)
    modes = jnp.dot(sums, into_ref[...], precision=lax.Precision.HIGHEST, preferred_element_type=F32)
    packed = jnp.concatenate([modes[0:4, :], modes[4:8, :]], axis=1)
    send_ref[...] = jnp.broadcast_to(packed[None], send_ref.shape)
    copies += fetch([(send_ref, send_hbm)], sems, 3)
    edges = []
    for side, x in ((0, 0), (1, BX - 1)):
        at = slice(x, x + 1)
        ends = (rows_ref[4, at, :], rows_ref[6, at, :], rows_ref[7, at, :], rows_ref[5, at, :])
        edges.append(with_ends(c3_edges_ref[side] + added_ref[side, 0], row, ends))
    cnear_ref[...] = jnp.where(core == 0, edges[1], edges[0])
    cfar_ref[...] = jnp.where(core == 0, edges[0], edges[1])
    wait(copies)


def coarse_kernel(place_ref, got_ref, table_ref, own_ref, one_ref, two_ref, three_ref, rolled_ref, sums_ref):
    mate, group, gy = place_ref[1], place_ref[2], place_ref[3]
    turn = lax.rem(GY - gy, GY)
    for q in range(GROUPS):
        plane = lax.rem(group + q, GROUPS)
        for r in range(4):
            rolled_ref[q, r] = pltpu.roll(got_ref[plane, pl.ds(r, GY, stride=4), :], turn, 0)
    for m in range(OUT_X):
        totals = [jnp.zeros((8, 2 * CZ), F32)] * OUT_Y
        for q in range(GROUPS):
            away = jnp.abs(m - 1 - mate - MATES * q)
            away = jnp.minimum(away, jnp.abs(CX - away))
            source = [rolled_ref[q, r] for r in range(4)]
            weight = [table_ref[away, t] for t in range(OUT_Y + 3)]
            for j in range(OUT_Y):
                for r in range(4):
                    totals[j] = totals[j] + weight[j + 3 - r] * source[r]
        for j in range(OUT_Y):
            sums_ref[m, j : j + 1, :] = jnp.sum(totals[j], axis=0, keepdims=True)
    for flip, out in enumerate((own_ref, one_ref, two_ref, three_ref)):
        first = lax.bitwise_xor(mate, flip)
        for m in range(3):
            out[m * OUT_Y : (m + 1) * OUT_Y, :] = sums_ref[first + m]


def last_kernel(
    core_ref, own_ref, one_ref, two_ref, three_ref, out_table_ref, c3_ref, base_ref, inverse_ref, planes_ref, added_ref, rows_ref, cnear_ref, cfar_ref,
    out_hbm, w_ref, out_ref, sems,
):
    core = core_ref[0]
    modes = (own_ref[...] + one_ref[...]) + (two_ref[...] + three_ref[...])
    coarse = jnp.dot(modes, out_table_ref[...], precision=lax.Precision.HIGHEST, preferred_element_type=F32)
    low, middle, high = (coarse[m * OUT_Y : (m + 1) * OUT_Y, :] for m in range(3))

    def rows_of(plane):
        return jnp.concatenate([jnp.broadcast_to(plane[j : j + 1, :], (8, NZ)) for j in range(1, OUT_Y - 1)], 0)

    def side_sum(plane, fine):
        return shifted_sum(fine, plane[0:1, :], plane[OUT_Y - 1 : OUT_Y, :]) + zsum(fine)

    s, s_low, s_high = rows_of(middle), rows_of(low), rows_of(high)
    beside = side_sum(middle, s)
    row = lax.broadcasted_iota(jnp.int32, (8, NZ), 0)
    none = jnp.zeros((1, NZ), F32)
    added_at = {0: (0, 0), 1: (0, 1), BX - 2: (1, 1), BX - 1: (1, 0)}
    for side, fine, plane in ((0, s_low, low), (1, s_high, high)):
        beyond = jnp.where((core == 0) == (side == 1), cnear_ref[...], cfar_ref[...])
        value = beyond + fine + s + side_sum(plane, fine)
        w_ref[(BX + 1) * side] = w2 * (planes_ref[side] * value - fine)
    y_w = []
    for side, edge, near_edge in ((0, 0, 1), (1, OUT_Y - 1, OUT_Y - 2)):
        fine = jnp.broadcast_to(middle[edge : edge + 1, :], (BX, NZ))
        value = rows_ref[side] + fine + middle[near_edge : near_edge + 1, :] + zsum(fine)
        value = value + shifted_sum(fine, low[edge : edge + 1, :], high[edge : edge + 1, :])
        y_w.append(w2 * (rows_ref[2 + side] * value - fine))
    for x in range(BX):
        around = beside + (s_low if x == 0 else s) + (s_high if x == BX - 1 else s)
        at = slice(x, x + 1)
        ends = (rows_ref[4, at, :], rows_ref[6, at, :], rows_ref[7, at, :], rows_ref[5, at, :])
        c3 = with_ends(c3_ref[x], row, ends)
        if x in added_at:
            c3 = c3 + added_ref[added_at[x]]
        w_ref[x + 1] = w2 * (inverse_ref[x] * (c3 + around) - s)
    copies = []
    for x in range(BX):
        w = w_ref[x + 1]
        near = w_ref[x] + w_ref[x + 2] + zsum(w)
        near = near + shifted_sum(w, y_w[0][x : x + 1, :], y_w[1][x : x + 1, :])
        base = with_ends(base_ref[x], row, (rows_ref[6, x : x + 1, :], none, none, rows_ref[7, x : x + 1, :]))
        if x in (0, BX - 1):
            base = base + added_ref[0 if x == 0 else 1, 1]
        out_ref[x] = base + s + w + w1 * ((1.0 - w2) / w2 * w + inverse_ref[x] * near)
        copies += fetch([(out_ref.at[x], out_hbm.at[x])], sems, x)
    wait(copies)


def call(kernel, outs, ins, in_specs, out_specs, scratch=(), sems=0, cost=None, aliases=None):
    scratch = [pltpu.VMEM(shape, F32) for shape in scratch]
    if sems:
        scratch.append(pltpu.SemaphoreType.DMA((sems,)))
    ins = [
        x if spec is SMEM else pltpu.with_memory_space_constraint(x, spec.memory_space)
        for x, spec in zip(ins, in_specs)
    ]
    return pl.pallas_call(
        kernel,
        out_shape=[spec.memory_space(shape, F32) for shape, spec in zip(outs, out_specs)],
        in_specs=in_specs,
        out_specs=out_specs,
        scratch_shapes=scratch,
        cost_estimate=cost,
        input_output_aliases=aliases or {},
        compiler_params=pltpu.CompilerParams(vmem_limit_bytes=12 * 1024 * 1024),
    )(*ins)


def hold_kernel(*refs):
    pass


def body(cotangent, coefficient):
    table, into, out_table = tables()
    along_x = ("x", "pair", "chip", "core")
    core = lax.axis_index("core")
    mate = lax.axis_index("chip") * 2 + core
    place = jnp.stack([core, mate, lax.axis_index("x") * 2 + lax.axis_index("pair"), lax.axis_index("gy")])
    place = place.astype(jnp.int32)
    near_pairs = [(i, i ^ 1) for i in range(GX)]
    far_pairs = [(i, (i + 1) % GX if i % 2 else (i - 1) % GX) for i in range(GX)]
    up = [(i, (i + 1) % GY) for i in range(GY)]
    down = [(i, (i - 1) % GY) for i in range(GY)]

    def near_swap(v):
        return lax.ppermute(v, along_x, near_pairs)

    def far_swap(v):
        return lax.ppermute(v, along_x, far_pairs)

    brick, plane = (BX, BY, NZ), (BY, NZ)
    tiny_near, tiny_far, y_low, y_high = call(
        strip_kernel,
        [(8, NZ), (8, NZ), (34, NZ), (34, NZ)],
        [place, cotangent, coefficient],
        [SMEM, HBM, HBM],
        [VMEM] * 4,
        scratch=[(2, BX, 8, NZ), (2, BX, 8, NZ)],
        sems=4,
    )
    tiny_far, tiny_near = far_swap(tiny_far), near_swap(tiny_near)
    near, far = call(
        edge_kernel,
        [(3,) + plane, (3,) + plane],
        [place, cotangent, coefficient, tiny_near],
        [SMEM, VMEM, VMEM, VMEM],
        [VMEM] * 2,
    )
    far, near = far_swap(far), near_swap(near)
    corner_low = jnp.where(core == 0, tiny_far, tiny_near)
    corner_high = jnp.where(core == 0, tiny_near, tiny_far)
    y_low = jnp.concatenate([y_low[:32], corner_low[:4], corner_high[:4], y_low[32:]], 0)
    y_high = jnp.concatenate([y_high[:32], corner_low[4:], corner_high[4:], y_high[32:]], 0)
    from_low = lax.ppermute(y_high, "gy", up)
    from_high = lax.ppermute(y_low, "gy", down)
    edge_planes = (2,) + plane
    w5_edges, inverse_edges, c3_edges, own_rows, sums, c3, base, inverse = call(
        local_kernel,
        [edge_planes, edge_planes, edge_planes, (6, BX, NZ), (8, NZ), brick, brick, brick],
        [cotangent, coefficient],
        [VMEM] * 2,
        [VMEM] * 6 + [HBM] * 2,
        scratch=[brick] * 4,
        sems=2,
        cost=pl.CostEstimate(flops=40 * BX * BY * NZ, bytes_accessed=5 * 4 * BX * BY * NZ, transcendentals=0),
    )
    rows, c_near, c_far, added, send, planes, c3 = call(
        first_kernel,
        [(8, BX, NZ), plane, plane, (2,) + edge_planes, (GROUPS * GY, 4, 2 * CZ), edge_planes, brick],
        [place, w5_edges, inverse_edges, c3_edges, own_rows, sums, c3, near, far, from_low, from_high, jnp.asarray(into)],
        [SMEM] + [VMEM] * 11,
        [VMEM] * 4 + [HBM] * 3,
        scratch=[(GROUPS * GY, 4, 2 * CZ)],
        sems=4,
    )
    got = lax.all_to_all(send, ("x", "pair", "gy"), 0, 0, tiled=True)
    c_near, c_far = near_swap(c_near), far_swap(c_far)
    table = jnp.asarray(table)
    got, c3, base, inverse, planes = call(
        hold_kernel,
        [got.shape, brick, brick, brick, edge_planes],
        [got, c3, base, inverse, planes, table],
        [VMEM] + [HBM] * 4 + [VMEM],
        [VMEM] + [HBM] * 4,
        aliases={i: i for i in range(5)},
    )
    own, one, two, three = call(
        coarse_kernel,
        [(3 * OUT_Y, 2 * CZ)] * 4,
        [place, got.reshape(GROUPS, ROWS, 2 * CZ), table],
        [SMEM, VMEM, VMEM],
        [VMEM] * 4,
        scratch=[(GROUPS, 4, GY, 2 * CZ), (OUT_X, OUT_Y, 2 * CZ)],
        cost=pl.CostEstimate(flops=10**11, bytes_accessed=10**7, transcendentals=0),
    )
    one, two, three = (
        lax.ppermute(v, along_x, [(i, i ^ flip) for i in range(GX)]) for flip, v in ((1, one), (2, two), (3, three))
    )
    return call(
        last_kernel,
        [brick],
        [place, own, one, two, three, jnp.asarray(out_table), c3, base, inverse, planes, added, rows, c_near, c_far],
        [SMEM] + [VMEM] * 13,
        [HBM],
        scratch=[(BX + 2,) + plane, brick],
        sems=BX,
    )[0]


def solution(mesh):
    split = Mesh(np.asarray(mesh.devices).reshape(4, 2, 2, 2, GY), ("x", "pair", "chip", "core", "gy"))
    spec = P(("x", "pair", "chip", "core"), "gy", None)
    return jax.shard_map(body, mesh=split, in_specs=(spec, spec), out_specs=spec, check_vma=False)
```

```python
import math

import jax
import jax.numpy as jnp
import numpy as np
from jax import lax
from jax.experimental import pallas as pl
from jax.experimental.pallas import tpu as pltpu
from jax.sharding import Mesh
from jax.sharding import PartitionSpec as P

screen = 0.02
w1 = 1.0 / (1.25 + 0.75 * math.cos(math.pi / 4.0))
w2 = 1.0 / (1.25 - 0.75 * math.cos(math.pi / 4.0))

BX, BY, NZ = 8, 64, 512
CX, CY, CZ = 32, 64, 64
GX, GY = 32, 8
MATES = 4
GROUPS = GX // MATES
ROWS = CY // 2
OUT_Y = BY // 8 + 2
OUT_X = MATES + 2

VMEM = pl.BlockSpec(memory_space=pltpu.VMEM)
HBM = pl.BlockSpec(memory_space=pltpu.HBM)
F32 = jnp.float32


def basis():
    place = np.arange(CZ)
    columns, freq = [], []
    for k in range(CZ // 2 + 1):
        scale = math.sqrt((1.0 if k in (0, CZ // 2) else 2.0) / CZ)
        columns.append(scale * np.cos(2.0 * math.pi * k * place / CZ))
        freq.append(k)
    for k in range(1, CZ // 2):
        columns.append(math.sqrt(2.0 / CZ) * np.sin(2.0 * math.pi * k * place / CZ))
        freq.append(k)
    return np.stack(columns, 1), np.array(freq)


def symbol(length):
    return 2.0 - 2.0 * np.cos(2.0 * math.pi * np.arange(length) / length)


def tables():
    columns, freq = basis()
    spectrum = (
        screen
        + symbol(CX)[:, None, None]
        + symbol(CY)[None, :, None]
        + symbol(CZ)[freq][None, None, :]
    )
    green = np.real(np.fft.ifft2(1.0 / spectrum, axes=(0, 1)))
    t, d, h = np.meshgrid(np.arange(OUT_Y + 3), np.arange(GY), np.arange(2), indexing="ij")
    shift = (t - 4 - 8 * d - 4 * h) % CY
    table = green[: CX // 2 + 1][:, shift].reshape(CX // 2 + 1, OUT_Y + 3, GY, 2 * CZ)
    table = table.astype(np.float32)
    into = np.repeat(columns, NZ // CZ, axis=0).astype(np.float32)
    out = np.concatenate([into.T, into.T], 0) / 8.0
    return table, into, out.astype(np.float32)


def zsum(v):
    return pltpu.roll(v, 1, 1) + pltpu.roll(v, NZ - 1, 1)


def shifted_sum(v, low, high):
    size = v.shape[0]
    row = lax.broadcasted_iota(jnp.int32, v.shape, 0)
    before = jnp.where(row == 0, low, pltpu.roll(v, 1, 0))
    after = jnp.where(row == size - 1, high, pltpu.roll(v, size - 1, 0))
    return before + after


def fetch(pairs, sems, first=0):
    copies = [pltpu.make_async_copy(s, d, sems.at[first + i]) for i, (s, d) in enumerate(pairs)]
    for copy in copies:
        copy.start()
    return copies


def wait(copies):
    for copy in copies:
        copy.wait()


def strip_kernel(cot_hbm, coef_hbm, tnear_ref, tfar_ref, ylow_ref, yhigh_ref, cot_ref, coef_ref, sems):
    core = lax.axis_index("core")
    ends = (pl.ds(0, 8), pl.ds(BY - 8, 8))
    wait(
        fetch(
            [(hbm.at[:, ends[i], :], ref.at[i]) for i in range(2) for hbm, ref in ((cot_hbm, cot_ref), (coef_hbm, coef_ref))],
            sems,
        )
    )
    for side, out in ((0, ylow_ref), (1, yhigh_ref)):
        order = (0, 1, 2) if side == 0 else (7, 6, 5)
        cot = [cot_ref[side, :, r, :] for r in order]
        inverse = [1.0 / (6.0 + coef_ref[side, :, r, :]) for r in order]
        w5 = [w2 * v * i for v, i in zip(cot, inverse)]
        none = jnp.zeros((1, NZ), F32)
        kept = (1.0 - w2) * cot[0] + w5[1]
        out[0:8, :] = w5[0]
        out[8:16, :] = inverse[0]
        out[16:24, :] = kept
        c4 = (1.0 - w2) * cot[1] + w5[0] + w5[2] + zsum(w5[1]) + shifted_sum(w5[1], none, none)
        out[24:32, :] = w1 * inverse[1] * c4
        out[32:33, :] = inverse[1][0:1, :]
        out[33:34, :] = inverse[1][7:8, :]

        def corner(edge, inner):
            at = slice(edge, edge + 1)
            return w5[0][at], inverse[0][at], kept[at] + w5[0][inner : inner + 1], w5[1][at]

        for i, (low, high) in enumerate(zip(corner(0, 1), corner(BX - 1, BX - 2))):
            place = slice(4 * side + i, 4 * side + i + 1)
            tnear_ref[place, :] = jnp.where(core == 0, high, low)
            tfar_ref[place, :] = jnp.where(core == 0, low, high)


def edge_kernel(cot_ref, coef_ref, after_ref, near_ref, far_ref):
    core = lax.axis_index("core")
    for out, edge, step in (
        (far_ref, (BX - 1) * core, 1 - 2 * core),
        (near_ref, (BX - 1) * (1 - core), 2 * core - 1),
    ):
        cot = cot_ref[edge]
        inverse = 1.0 / (6.0 + coef_ref[edge])
        out[0] = w2 * cot * inverse
        out[1] = inverse
        out[2] = (1.0 - w2) * cot + w2 * cot_ref[edge + step] / (6.0 + coef_ref[edge + step])


def local_kernel(
    cot_ref, coef_ref,
    w5_edges_ref, inverse_edges_ref, c3_edges_ref, rows_ref, sums_ref, c3_ref, base_hbm, inverse_hbm,
    w5_ref, inverse_ref, w4_ref, base_ref, sems,
):
    none = jnp.zeros((1, NZ), F32)
    for x in range(BX):
        inverse = 1.0 / (6.0 + coef_ref[x])
        inverse_ref[x] = inverse
        w5_ref[x] = w2 * cot_ref[x] * inverse
    copies = fetch([(inverse_ref, inverse_hbm)], sems)
    for x in range(BX):
        w5 = w5_ref[x]
        c4 = (1.0 - w2) * cot_ref[x] + zsum(w5) + shifted_sum(w5, none, none)
        if x > 0:
            c4 = c4 + w5_ref[x - 1]
        if x < BX - 1:
            c4 = c4 + w5_ref[x + 1]
        w4 = w1 * inverse_ref[x] * c4
        w4_ref[x] = w4
        base_ref[x] = w5 + w4
        c3_ref[x] = (1.0 - w1) * c4
    copies += fetch([(base_ref, base_hbm)], sems, 1)
    total = jnp.zeros((BY, NZ), F32)
    for x in range(BX):
        w4 = w4_ref[x]
        c3 = c3_ref[x] + zsum(w4) + shifted_sum(w4, none, none)
        if x > 0:
            c3 = c3 + w4_ref[x - 1]
        if x < BX - 1:
            c3 = c3 + w4_ref[x + 1]
        c3_ref[x] = c3
        total = total + c3
    sums_ref[...] = jnp.sum(total.reshape(BY // 8, 8, NZ), axis=1)
    for side, x, y in ((0, 0, 0), (1, BX - 1, BY - 1)):
        w5_edges_ref[side] = w5_ref[x]
        inverse_edges_ref[side] = inverse_ref[x]
        c3_edges_ref[side] = c3_ref[x]
        rows_ref[side] = w5_ref[:, y, :]
        rows_ref[2 + side] = inverse_ref[:, y, :]
        rows_ref[4 + side] = w4_ref[:, y, :]
    wait(copies)


def with_ends(plane, row, ends):
    low = jnp.where(row == 0, ends[0], jnp.where(row == 1, ends[1], 0.0))
    high = jnp.where(row == 6, ends[2], jnp.where(row == 7, ends[3], 0.0))
    return jnp.concatenate([plane[0:8, :] + low, plane[8 : BY - 8, :], plane[BY - 8 : BY, :] + high], 0)


def first_kernel(
    w5_edges_ref, inverse_edges_ref, c3_edges_ref, own_rows_ref, part_sums_ref, c3_ref,
    near_ref, far_ref, ylow_ref, yhigh_ref, into_ref,
    rows_ref, cnear_ref, cfar_ref, added_ref, send_hbm, planes_hbm, c3_hbm,
    send_ref, sems,
):
    core = lax.axis_index("core")
    copies = fetch(
        [
            (c3_ref, c3_hbm),
            (near_ref.at[1], planes_hbm.at[1 - core]),
            (far_ref.at[1], planes_hbm.at[core]),
        ],
        sems,
    )
    none = jnp.zeros((1, NZ), F32)
    row = lax.broadcasted_iota(jnp.int32, (8, NZ), 0)
    plane_total = jnp.zeros((BY, NZ), F32)
    for halo, side, at_high in ((near_ref, 1 - core, core == 0), (far_ref, core, core == 1)):
        low = jnp.where(at_high, ylow_ref[36:37, :], ylow_ref[32:33, :])
        high = jnp.where(at_high, yhigh_ref[36:37, :], yhigh_ref[32:33, :])
        w5 = halo[0]
        c4 = halo[2] + w5_edges_ref[side] + zsum(w5) + shifted_sum(w5, low, high)
        w4_added = w1 * inverse_edges_ref[side] * w5
        c3_added = (1.0 - w1) * w5 + w1 * halo[1] * c4 + zsum(w4_added) + shifted_sum(w4_added, none, none)
        added_ref[side, 0] = c3_added
        added_ref[side, 1] = w4_added
        plane_total = plane_total + c3_added + w4_added
    sums = part_sums_ref[...] + jnp.sum(plane_total.reshape(BY // 8, 8, NZ), axis=1)
    for side, packet, edge in ((0, ylow_ref, 0), (1, yhigh_ref, BY - 1)):
        w5, corners, inverse = packet[0:8, :], packet[32:40, :], packet[8:16, :]
        c4 = packet[16:24, :] + own_rows_ref[side] + zsum(w5)
        c4 = c4 + shifted_sum(w5, corners[0:1, :], corners[4:5, :])
        w4 = w1 * inverse * c4
        w4_added = w1 * own_rows_ref[2 + side] * w5
        c3_added = (1.0 - w1) * w5 + w4 + zsum(w4_added) + shifted_sum(w4_added, none, none)
        beside = zsum(corners)
        ends = []
        inner = own_rows_ref[4 + side] + w4_added
        beyond = packet[24:32, :]
        for i, at, x_side in ((0, 0, 0), (4, BX - 1, 1)):
            halo = jnp.where(
                (core == 0) == (x_side == 0), far_ref[0, edge : edge + 1, :], near_ref[0, edge : edge + 1, :]
            )
            c4_corner = corners[i + 2 : i + 3, :] + beside[i : i + 1, :] + w5[at : at + 1, :] + halo
            ends.append(w1 * corners[i + 1 : i + 2, :] * c4_corner)
            missing = w1 * packet[40 + x_side : 41 + x_side, :] * corners[i + 3 : i + 4, :]
            missing = missing + added_ref[x_side, 1, edge : edge + 1, :]
            beyond = beyond + jnp.where(row == at, missing, 0.0)
        rows_ref[side] = (1.0 - w1) * c4 + beyond + inner + zsum(w4) + shifted_sum(w4, *ends)
        rows_ref[2 + side] = inverse
        rows_ref[4 + side] = c3_added
        rows_ref[6 + side] = w4_added
        more = jnp.sum(c3_added + w4_added, axis=0, keepdims=True)
        sums = sums + jnp.where(row == 7 * side, more, 0.0)
    modes = jnp.dot(sums, into_ref[...], precision=lax.Precision.HIGHEST, preferred_element_type=F32)
    packed = jnp.concatenate([modes[0:4, :], modes[4:8, :]], axis=1)
    send_ref[...] = jnp.broadcast_to(packed[None], send_ref.shape)
    copies += fetch([(send_ref, send_hbm)], sems, 3)
    edges = []
    for side, x in ((0, 0), (1, BX - 1)):
        at = slice(x, x + 1)
        ends = (rows_ref[4, at, :], rows_ref[6, at, :], rows_ref[7, at, :], rows_ref[5, at, :])
        edges.append(with_ends(c3_edges_ref[side] + added_ref[side, 0], row, ends))
    cnear_ref[...] = jnp.where(core == 0, edges[1], edges[0])
    cfar_ref[...] = jnp.where(core == 0, edges[0], edges[1])
    wait(copies)


def coarse_kernel(got_ref, table_ref, own_ref, one_ref, two_ref, three_ref, rolled_ref, sums_ref):
    mate = lax.axis_index("chip") * 2 + lax.axis_index("core")
    group = lax.axis_index("x") * 2 + lax.axis_index("pair")
    gy = lax.axis_index("gy")
    turn = lax.rem(GY - gy, GY)
    for q in range(GROUPS):
        plane = lax.rem(group + q, GROUPS)
        for r in range(4):
            rolled_ref[q, r] = pltpu.roll(got_ref[plane, pl.ds(r, GY, stride=4), :], turn, 0)
    for m in range(OUT_X):
        totals = [jnp.zeros((8, 2 * CZ), F32)] * OUT_Y
        for q in range(GROUPS):
            away = jnp.abs(m - 1 - mate - MATES * q)
            away = jnp.minimum(away, jnp.abs(CX - away))
            source = [rolled_ref[q, r] for r in range(4)]
            weight = [table_ref[away, t] for t in range(OUT_Y + 3)]
            for j in range(OUT_Y):
                for r in range(4):
                    totals[j] = totals[j] + weight[j + 3 - r] * source[r]
        for j in range(OUT_Y):
            sums_ref[m, j : j + 1, :] = jnp.sum(totals[j], axis=0, keepdims=True)
    for flip, out in enumerate((own_ref, one_ref, two_ref, three_ref)):
        first = lax.bitwise_xor(mate, flip)
        for m in range(3):
            out[m * OUT_Y : (m + 1) * OUT_Y, :] = sums_ref[first + m]


def last_kernel(
    own_ref, one_ref, two_ref, three_ref, out_table_ref, c3_ref, base_ref, inverse_ref, planes_ref, added_ref, rows_ref, cnear_ref, cfar_ref,
    out_hbm, w_ref, out_ref, sems,
):
    core = lax.axis_index("core")
    modes = (own_ref[...] + one_ref[...]) + (two_ref[...] + three_ref[...])
    coarse = jnp.dot(modes, out_table_ref[...], precision=lax.Precision.HIGHEST, preferred_element_type=F32)
    low, middle, high = (coarse[m * OUT_Y : (m + 1) * OUT_Y, :] for m in range(3))

    def rows_of(plane):
        return jnp.concatenate([jnp.broadcast_to(plane[j : j + 1, :], (8, NZ)) for j in range(1, OUT_Y - 1)], 0)

    def side_sum(plane, fine):
        return shifted_sum(fine, plane[0:1, :], plane[OUT_Y - 1 : OUT_Y, :]) + zsum(fine)

    s, s_low, s_high = rows_of(middle), rows_of(low), rows_of(high)
    beside = side_sum(middle, s)
    row = lax.broadcasted_iota(jnp.int32, (8, NZ), 0)
    none = jnp.zeros((1, NZ), F32)
    added_at = {0: (0, 0), 1: (0, 1), BX - 2: (1, 1), BX - 1: (1, 0)}
    for side, fine, plane in ((0, s_low, low), (1, s_high, high)):
        beyond = jnp.where((core == 0) == (side == 1), cnear_ref[...], cfar_ref[...])
        value = beyond + fine + s + side_sum(plane, fine)
        w_ref[(BX + 1) * side] = w2 * (planes_ref[side] * value - fine)
    y_w = []
    for side, edge, near_edge in ((0, 0, 1), (1, OUT_Y - 1, OUT_Y - 2)):
        fine = jnp.broadcast_to(middle[edge : edge + 1, :], (BX, NZ))
        value = rows_ref[side] + fine + middle[near_edge : near_edge + 1, :] + zsum(fine)
        value = value + shifted_sum(fine, low[edge : edge + 1, :], high[edge : edge + 1, :])
        y_w.append(w2 * (rows_ref[2 + side] * value - fine))
    for x in range(BX):
        around = beside + (s_low if x == 0 else s) + (s_high if x == BX - 1 else s)
        at = slice(x, x + 1)
        ends = (rows_ref[4, at, :], rows_ref[6, at, :], rows_ref[7, at, :], rows_ref[5, at, :])
        c3 = with_ends(c3_ref[x], row, ends)
        if x in added_at:
            c3 = c3 + added_ref[added_at[x]]
        w_ref[x + 1] = w2 * (inverse_ref[x] * (c3 + around) - s)
    copies = []
    for x in range(BX):
        w = w_ref[x + 1]
        near = w_ref[x] + w_ref[x + 2] + zsum(w)
        near = near + shifted_sum(w, y_w[0][x : x + 1, :], y_w[1][x : x + 1, :])
        base = with_ends(base_ref[x], row, (rows_ref[6, x : x + 1, :], none, none, rows_ref[7, x : x + 1, :]))
        if x in (0, BX - 1):
            base = base + added_ref[0 if x == 0 else 1, 1]
        out_ref[x] = base + s + w + w1 * ((1.0 - w2) / w2 * w + inverse_ref[x] * near)
        copies += fetch([(out_ref.at[x], out_hbm.at[x])], sems, x)
    wait(copies)


def call(kernel, outs, ins, in_specs, out_specs, scratch=(), sems=0, cost=None, aliases=None):
    scratch = [pltpu.VMEM(shape, F32) for shape in scratch]
    if sems:
        scratch.append(pltpu.SemaphoreType.DMA((sems,)))
    ins = [
        pltpu.with_memory_space_constraint(x, spec.memory_space) for x, spec in zip(ins, in_specs)
    ]
    return pl.pallas_call(
        kernel,
        out_shape=[spec.memory_space(shape, F32) for shape, spec in zip(outs, out_specs)],
        in_specs=in_specs,
        out_specs=out_specs,
        scratch_shapes=scratch,
        cost_estimate=cost,
        input_output_aliases=aliases or {},
        compiler_params=pltpu.CompilerParams(vmem_limit_bytes=12 * 1024 * 1024),
    )(*ins)


def hold_kernel(*refs):
    pass


def body(cotangent, coefficient):
    table, into, out_table = tables()
    along_x = ("x", "pair", "chip", "core")
    core = lax.axis_index("core")
    near_pairs = [(i, i ^ 1) for i in range(GX)]
    far_pairs = [(i, (i + 1) % GX if i % 2 else (i - 1) % GX) for i in range(GX)]
    up = [(i, (i + 1) % GY) for i in range(GY)]
    down = [(i, (i - 1) % GY) for i in range(GY)]

    def near_swap(v):
        return lax.ppermute(v, along_x, near_pairs)

    def far_swap(v):
        return lax.ppermute(v, along_x, far_pairs)

    brick, plane = (BX, BY, NZ), (BY, NZ)
    tiny_near, tiny_far, y_low, y_high = call(
        strip_kernel,
        [(8, NZ), (8, NZ), (34, NZ), (34, NZ)],
        [cotangent, coefficient],
        [HBM, HBM],
        [VMEM] * 4,
        scratch=[(2, BX, 8, NZ), (2, BX, 8, NZ)],
        sems=4,
    )
    tiny_far, tiny_near = far_swap(tiny_far), near_swap(tiny_near)
    near, far = call(
        edge_kernel,
        [(3,) + plane, (3,) + plane],
        [cotangent, coefficient, tiny_near],
        [VMEM, VMEM, VMEM],
        [VMEM] * 2,
    )
    far, near = far_swap(far), near_swap(near)
    corner_low = jnp.where(core == 0, tiny_far, tiny_near)
    corner_high = jnp.where(core == 0, tiny_near, tiny_far)
    y_low = jnp.concatenate([y_low[:32], corner_low[:4], corner_high[:4], y_low[32:]], 0)
    y_high = jnp.concatenate([y_high[:32], corner_low[4:], corner_high[4:], y_high[32:]], 0)
    from_low = lax.ppermute(y_high, "gy", up)
    from_high = lax.ppermute(y_low, "gy", down)
    edge_planes = (2,) + plane
    w5_edges, inverse_edges, c3_edges, own_rows, sums, c3, base, inverse = call(
        local_kernel,
        [edge_planes, edge_planes, edge_planes, (6, BX, NZ), (8, NZ), brick, brick, brick],
        [cotangent, coefficient],
        [VMEM] * 2,
        [VMEM] * 6 + [HBM] * 2,
        scratch=[brick] * 4,
        sems=2,
        cost=pl.CostEstimate(flops=40 * BX * BY * NZ, bytes_accessed=5 * 4 * BX * BY * NZ, transcendentals=0),
    )
    rows, c_near, c_far, added, send, planes, c3 = call(
        first_kernel,
        [(8, BX, NZ), plane, plane, (2,) + edge_planes, (GROUPS * GY, 4, 2 * CZ), edge_planes, brick],
        [w5_edges, inverse_edges, c3_edges, own_rows, sums, c3, near, far, from_low, from_high, jnp.asarray(into)],
        [VMEM] * 11,
        [VMEM] * 4 + [HBM] * 3,
        scratch=[(GROUPS * GY, 4, 2 * CZ)],
        sems=4,
    )
    got = lax.all_to_all(send, ("x", "pair", "gy"), 0, 0, tiled=True)
    c_near, c_far = near_swap(c_near), far_swap(c_far)
    table = jnp.asarray(table)
    got, c3, base, inverse, planes = call(
        hold_kernel,
        [got.shape, brick, brick, brick, edge_planes],
        [got, c3, base, inverse, planes, table],
        [VMEM] + [HBM] * 4 + [VMEM],
        [VMEM] + [HBM] * 4,
        aliases={i: i for i in range(5)},
    )
    own, one, two, three = call(
        coarse_kernel,
        [(3 * OUT_Y, 2 * CZ)] * 4,
        [got.reshape(GROUPS, ROWS, 2 * CZ), table],
        [VMEM, VMEM],
        [VMEM] * 4,
        scratch=[(GROUPS, 4, GY, 2 * CZ), (OUT_X, OUT_Y, 2 * CZ)],
        cost=pl.CostEstimate(flops=10**11, bytes_accessed=10**7, transcendentals=0),
    )
    one, two, three = (
        lax.ppermute(v, along_x, [(i, i ^ flip) for i in range(GX)]) for flip, v in ((1, one), (2, two), (3, three))
    )
    return call(
        last_kernel,
        [brick],
        [own, one, two, three, jnp.asarray(out_table), c3, base, inverse, planes, added, rows, c_near, c_far],
        [VMEM] * 13,
        [HBM],
        scratch=[(BX + 2,) + plane, brick],
        sems=BX,
    )[0]


def solution(mesh):
    split = Mesh(np.asarray(mesh.devices).reshape(4, 2, 2, 2, GY), ("x", "pair", "chip", "core", "gy"))
    spec = P(("x", "pair", "chip", "core"), "gy", None)
    return jax.shard_map(body, mesh=split, in_specs=(spec, spec), out_specs=spec, check_vma=False)
```
